32 devices in a mesh: expert: 8 (over z, y), shard: 4 (over x, core).
Axes of the slice: x: 2, y: 2, z: 4, core: 2. Of those that a mesh axis runs over, the one named last changes fastest.
Arguments:
- tokens: bfloat16 [8192, 768], P(('expert', 'shard')), may hold values from -6 to 6
- norm1_gain: float32 [768], replicated, may hold values from 0.5 to 1.5
- qkv_weight: bfloat16 [3, 768, 768], P(None, None, 'shard'), may hold values from -0.21875 to 0.21875
- out_weight: bfloat16 [768, 768], P('shard'), may hold values from -1.25 to 1.25
- bucket_position_bias: float32 [32, 12], P(None, 'shard'), may hold values from -4 to 4
- norm2_gain: float32 [768], replicated, may hold values from 0.5 to 1.5
- router_weight: float32 [768, 8], replicated, may hold values from -0.109375 to 0.109375
- expert_in: bfloat16 [8, 768, 3072], P('expert', None, 'shard'), may hold values from -0.3125 to 0.3125
- expert_out: bfloat16 [8, 3072, 768], P('expert', 'shard'), may hold values from -0.875 to 0.875
- segment: int32 [8192], P('expert'), may hold values from 0 to 258, as said below
- route: int32 [8192], P(('expert', 'shard')), may hold values from 0 to 7
- slot: int32 [8192], P(('expert', 'shard')), may hold values from -1 to 39, as said below
- cotangent: bfloat16 [8192, 768], P(('expert', 'shard')), may hold values from -6 to 6
Outputs:
- output: bfloat16 [8192, 768], P(('expert', 'shard'))
- tokens_grad: float32 [8192, 768], P(('expert', 'shard'))
- norm1_gain_grad: float32 [768], replicated
- qkv_weight_grad: float32 [3, 768, 768], P(None, None, 'shard')
- output_weight_gradient: float32 [768, 768], P('shard')
- position_bias_grad: float32 [32, 12], P(None, 'shard')
- norm2_gain_grad: float32 [768], replicated
- router_weight_grad: float32 [768, 8], replicated
- expert_in_grad: float32 [8, 768, 3072], P('expert', None, 'shard')
- expert_out_grad: float32 [8, 3072, 768], P('expert', 'shard')
The draws below stay inside these ranges and needn't reach their ends.
Inputs may be any that keep to these rules, and one draw needn't show every extreme that they name: `segment`: segment numbers never fall along a sequence of 1024 tokens; only equality within one sequence has meaning. slot is the token's rank, in order of position, among the tokens of its block of 256 with the same route, or -1 where that rank is 40 or more.
All inputs are finite; a program needn't handle non-finite values.
Results may differ from the reference program's by a relative error of at most 0.015.
Values may be sent and summed in bfloat16 or wider, within the bound.
No kernel may reach another device: no remote copies, remote signals or barrier semaphores. Data moves between devices by JAX's collectives and lax.ppermute only.
A program may use at most 128 MiB of HBM per device.

```python
import jax
import jax.numpy as jnp
from jax import lax

D = 768
HEADS = 12
HEAD_DIM = 64
FF = 3072
BUCKETS = 32
TOK_DEV = 256
EXPERTS = 8
SEQ_LEN = 1024
TOKENS = 8192
CAPACITY = 40


def routing(key):
    blocks = TOKENS // TOK_DEV
    capacity = (5 * TOK_DEV + 4 * EXPERTS - 1) // (4 * EXPERTS)
    first, second, third, fourth_part = jax.random.split(key, 4)
    order = jax.random.permutation(first, EXPERTS)
    weights = 1 + 3 * (order < max(1, EXPERTS // 8)).astype(jnp.int32)
    bounds = jnp.cumsum(weights)
    pick = jax.random.randint(second, (TOKENS,), 0, bounds[-1])
    route = jnp.sum((pick[:, None] >= bounds[None, :]).astype(jnp.int32), axis=1).astype(jnp.int32)
    hottest = jax.random.randint(third, (blocks, 1), 0, EXPERTS)
    block_keys = jax.random.split(fourth_part, blocks)
    ranks = jax.vmap(lambda single: jax.random.permutation(single, TOK_DEV))(block_keys)
    route = jnp.where(ranks < capacity + 1, hottest, route.reshape(blocks, TOK_DEV))
    expert_indicator = (route[:, :, None] == jnp.arange(EXPERTS, dtype=jnp.int32)[None, None, :]).astype(jnp.int32)
    position_rank = jnp.sum((jnp.cumsum(expert_indicator, axis=1) - 1) * expert_indicator, axis=2)
    slot = jnp.where(position_rank < capacity, position_rank, -1)
    return (route.reshape(TOKENS).astype(jnp.int32), slot.reshape(TOKENS).astype(jnp.int32))


def draw_route(key, part):
    shared = routing(key)
    return shared[0]


def draw_slot(key, part):
    shared = routing(key)
    return shared[1]


def draw_segment(key, part):
    key = jax.random.fold_in(key, 5)
    sequences = TOKENS // SEQ_LEN
    first, second, third = jax.random.split(key, 3)
    begin = jax.random.randint(first, (sequences, 1), 0, TOK_DEV // 2)
    finish = jax.random.randint(second, (sequences, 1), SEQ_LEN - TOK_DEV // 2 + 1, SEQ_LEN + 1)
    position = jnp.arange(SEQ_LEN, dtype=jnp.int32)[None, :]
    spots = jax.random.randint(third, (sequences, SEQ_LEN), 0, 32) == 0
    outside = (position < begin) | (position > finish)
    flags = spots & outside | (position == begin) | (position == finish)
    flags = flags & (position > 0)
    segment = jnp.cumsum(flags.astype(jnp.int32), axis=1)
    last_row = jnp.arange(sequences, dtype=jnp.int32)[:, None] == sequences - 1
    offset = jnp.where(last_row, TOK_DEV + 2 - segment[:, -1:], 0)
    segment = segment + offset
    return segment.reshape(TOKENS).astype(jnp.int32)


def shard_levels(rng, dims, cuts, least, top_value):
    def one(axis_at, shards_of):
        heights = jax.random.uniform(jax.random.fold_in(jax.random.fold_in(rng, 6), axis_at), (shards_of,), jnp.float32, least / len(cuts), top_value / len(cuts))
        return jnp.repeat(jnp.exp(heights), dims[axis_at] // shards_of).reshape((-1,) + (1,) * (len(dims) - axis_at - 1))

    loudness = one(*cuts[0])
    for cut in cuts[1:]:
        loudness = loudness * one(*cut)
    return loudness


def noise(stream_key, shape, scale, reach, cuts=(), kind=jnp.bfloat16):
    values = scale * jax.random.normal(stream_key, shape, jnp.float32)
    if cuts:
        values = values * shard_levels(stream_key, shape, cuts, -0.22, 0.18)
    return jnp.clip(values, -reach, reach).astype(kind)


def setup_inputs(seed: int = 0) -> dict:
    key_of = jax.random.split(jax.random.key(seed), 14)
    return {
        "tokens": noise(key_of[0], (TOKENS, D), 1.0, 6.0, ((0, 32),)),
        "norm1_gain": jnp.clip(1.0 + 0.1 * jax.random.normal(key_of[1], (D,), jnp.float32), 0.5, 1.5),
        "qkv_weight": noise(key_of[2], (3, D, D), D ** -0.5, 0.21875, ((2, 4),)),
        "out_weight": noise(key_of[3], (D, D), (D // 32) ** -0.5, 1.25, ((0, 4),)),
        "bucket_position_bias": noise(key_of[4], (BUCKETS, HEADS), 1.0, 4.0, ((1, 4),), jnp.float32),
        "norm2_gain": jnp.clip(1.0 + 0.1 * jax.random.normal(key_of[5], (D,), jnp.float32), 0.5, 1.5),
        "router_weight": noise(key_of[6], (D, EXPERTS), (4 * D) ** -0.5, 0.109375, (), jnp.float32),
        "expert_in": noise(key_of[7], (EXPERTS, D, FF), (D // 2) ** -0.5, 0.3125, ((0, 8), (2, 4))),
        "expert_out": noise(key_of[8], (EXPERTS, FF, D), (max(1, FF // (EXPERTS * EXPERTS))) ** -0.5, 0.875, ((0, 8), (1, 4))),
        "segment": draw_segment(jax.random.fold_in(key_of[13], 71), 0),
        "route": draw_route(jax.random.fold_in(key_of[13], 71), 0),
        "slot": draw_slot(jax.random.fold_in(key_of[13], 71), 0),
        "cotangent": noise(key_of[12], (TOKENS, D), 1.0, 6.0, ((0, 32),)),
    }


@jax.custom_vjp
def low(v):
    return lax.optimization_barrier(v.astype(jnp.bfloat16)).astype(jnp.float32)

@jax.custom_vjp
def low_back(v):
    return v

def low_keep(v):
    return (low(v), None)

def low_pass(kept, grad):
    return (grad,)

def back_keep(v):
    return (v, None)

def back_low(kept, grad):
    return (low(grad),)
low.defvjp(low_keep, low_pass)
low_back.defvjp(back_keep, back_low)
EPS = 1e-06
THRESHOLDS = (12, 16, 23, 32, 46, 64, 91)

def bucket_of(relative):
    distance = jnp.abs(relative).astype(jnp.int32)
    far = 8 + sum(((distance >= edge).astype(jnp.int32) for edge in THRESHOLDS))
    near = jnp.where(distance < 8, distance, jnp.minimum(far, 15))
    return (near + jnp.where(relative > 0, 16, 0)).astype(jnp.int32)

def rms_norm(values, gain):
    return values * lax.rsqrt(lax.optimization_barrier(jnp.mean(values * values, axis=-1, keepdims=True)) + EPS) * gain

def gelu_tanh(values):
    return jax.nn.gelu(values, approximate=True)

def reference(tokens, norm1_gain, qkv_weight, out_weight, bucket_position_bias, norm2_gain, router_weight, expert_in, expert_out, segment, route, slot, cotangent):
    highest_precision = lax.Precision.HIGHEST
    experts = EXPERTS
    capacity = CAPACITY
    blocks = TOKENS // TOK_DEV
    sequences = TOKENS // SEQ_LEN
    columns = jnp.arange(experts * capacity, dtype=jnp.int32)
    target = (route * capacity + slot).astype(jnp.int32)
    placed = (target[:, None] == columns[None, :]) & (slot[:, None] >= 0)
    dispatch = placed.astype(jnp.float32).reshape(blocks, TOK_DEV, experts * capacity)
    chosen = (route[:, None] == jnp.arange(experts, dtype=jnp.int32)[None, :]).astype(jnp.float32)
    position = jnp.arange(SEQ_LEN, dtype=jnp.int32)
    buckets = bucket_of(position[None, :] - position[:, None])
    segments = segment.reshape(sequences, SEQ_LEN)

    def forward(inputs, gain_one, qkv_w, out_w, table, gain_two, router_w, weight_in, weight_out):
        normed = low(rms_norm(inputs, gain_one))
        bias_terms = jnp.transpose(table[buckets], (2, 0, 1))

        def one_sequence(carry, pair):
            rows, segment_row_ids = pair
            projected = low(low_back(jnp.einsum('td,jde->jte', rows, qkv_w, precision=highest_precision)))
            queries = projected[0].reshape(SEQ_LEN, HEADS, HEAD_DIM)
            keys = projected[1].reshape(SEQ_LEN, HEADS, HEAD_DIM)
            values = projected[2].reshape(SEQ_LEN, HEADS, HEAD_DIM)
            scores = jnp.einsum('qhd,khd->hqk', queries, keys, precision=highest_precision) * 0.125 + bias_terms
            scores = low_back(scores)
            allowed = (segment_row_ids[:, None] == segment_row_ids[None, :])[None]
            scores = jnp.where(allowed, scores, -1000000000.0)
            probs = low(jax.nn.softmax(scores, axis=-1))
            mixed = low(low_back(jnp.einsum('hqk,khd->qhd', probs, values, precision=highest_precision)))
            attended = low_back(jnp.dot(mixed.reshape(SEQ_LEN, D), out_w, precision=highest_precision))
            return (carry, attended)
        start = jnp.zeros((), jnp.float32)
        _, attended = lax.scan(jax.checkpoint(one_sequence), start, (normed.reshape(sequences, SEQ_LEN, D), segments))
        hidden = inputs + attended.reshape(TOKENS, D)
        routed = low(rms_norm(hidden, gain_two))
        router_probs = jax.nn.softmax(jnp.dot(routed, router_w, precision=highest_precision), axis=-1)
        gate = lax.optimization_barrier(jnp.sum(router_probs * chosen, axis=-1))
        slot_rows = jnp.einsum('btx,btd->bxd', dispatch, routed.reshape(blocks, TOK_DEV, D), precision=highest_precision)
        slot_rows = jnp.transpose(slot_rows.reshape(blocks, experts, capacity, D), (1, 0, 2, 3)).reshape(experts, blocks * capacity, D)

        def one_expert(triple):
            rows, first, second = triple
            upward = low_back(jnp.dot(rows, first, precision=highest_precision))
            active = low(gelu_tanh(upward))
            return low(low_back(jnp.dot(active, second, precision=highest_precision)))
        produced = lax.map(jax.checkpoint(one_expert), (slot_rows, weight_in, weight_out))
        produced = jnp.transpose(produced.reshape(experts, blocks, capacity, D), (1, 0, 2, 3)).reshape(blocks, experts * capacity, D)
        combined = jnp.einsum('btx,bxd->btd', dispatch, produced, precision=highest_precision).reshape(TOKENS, D)
        return hidden + gate[:, None] * combined
    floats = (tokens.astype(jnp.float32), norm1_gain, qkv_weight.astype(jnp.float32), out_weight.astype(jnp.float32), bucket_position_bias, norm2_gain, router_weight, expert_in.astype(jnp.float32), expert_out.astype(jnp.float32))
    result, backward = jax.vjp(forward, *floats)
    grads = backward(cotangent.astype(jnp.float32))
    return (result.astype(jnp.bfloat16), grads[0], grads[1], grads[2], grads[3], grads[4], grads[5], grads[6], grads[7], grads[8])
```

```python
import functools

import jax
import jax.numpy as jnp
from jax import lax
from jax.experimental import pallas as pl
from jax.experimental.pallas import tpu as pltpu
from jax.sharding import PartitionSpec as P

D = 768
HEAD_DIM = 64
BUCKETS = 32


EPS = 1e-06
THRESHOLDS = (12, 16, 23, 32, 46, 64, 91)
NEG = -1000000000.0
F32 = jnp.float32
BF16 = jnp.bfloat16


def bucket_of(relative):
    distance = jnp.abs(relative)
    far = 8 + sum(((distance >= edge).astype(jnp.int32) for edge in THRESHOLDS))
    near = jnp.where(distance < 8, distance, jnp.minimum(far, 15))
    return near + jnp.where(relative > 0, 16, 0)


def rms_norm(values, gain):
    return values * lax.rsqrt(jnp.mean(values * values, axis=-1, keepdims=True) + EPS) * gain


def gelu_tanh(values):
    return jax.nn.gelu(values, approximate=True)


def dot(a, b, ca=1, cb=0):
    return lax.dot_general(a, b, (((ca,), (cb,)), ((), ())), preferred_element_type=F32)


def swap(x, axis, bit):
    size = lax.axis_size(axis)
    return lax.ppermute(x, axis, [(i, i ^ bit) for i in range(size)])


def after(x, *others):
    return lax.optimization_barrier((x, *others))[0]


def exchange(rows, last=None):
    size = lax.axis_size("expert")
    count = rows.shape[0] // size
    if size != 8:
        return lax.all_to_all(rows, "expert", split_axis=0, concat_axis=0, tiled=True)
    blocks = [rows[k * count : (k + 1) * count] for k in range(size)]
    got = blocks[:1] + [swap(blocks[k], "expert", k) for k in range(1, 4)]
    if last is not None:
        blocks[4:] = lax.optimization_barrier((*blocks[4:], got[1], *last))[:4]
    return jnp.concatenate(got + [swap(blocks[k], "expert", k) for k in range(4, size)])


def build_bias(table_ref, head, tiles_ref, tok):
    wide = 4 * tok
    row = lax.broadcasted_iota(jnp.int32, (8, wide), 0)
    col = lax.broadcasted_iota(jnp.int32, (8, wide), 1)
    relative = col - tok - row - jnp.where(col >= 3 * tok, wide, 0)
    bucket = bucket_of(relative)
    base = jnp.zeros((8, wide), F32)
    for b in range(BUCKETS):
        base = jnp.where(bucket == b, table_ref[b, head], base)
    for a in range(tok // 8):
        rows = pltpu.roll(base, 8 * a, 1) if a else base
        for d in range(3):
            tiles_ref[d + 1, 8 * a : 8 * a + 8, :] = rows[:, d * tok : (d + 1) * tok]
    tiles_ref[0] = jnp.full((tok, tok), table_ref[15, head], F32)
    tiles_ref[4] = jnp.full((tok, tok), table_ref[31, head], F32)


def tile_index(me, j, l):
    return jnp.clip((me ^ l) - (me ^ j), -2, 2) + 2


def masked_scores(me, j, q, keys, tiles_ref, seg_col, seg_row_ref, blocks, tok):
    parts = []
    for l in range(blocks):
        s = dot(q, keys[l * tok : (l + 1) * tok], 1, 1)
        s = s + tiles_ref[tile_index(me, j, l)]
        parts.append(jnp.where(seg_col == seg_row_ref[me ^ l], s, NEG))
    return parts


def forward_kernel(
    me_ref, table_ref, seg_row_ref, seg_col_ref, x0, x1, x2a, x2b, x3a, x3b, w_ref,
    proj_ref, lse_ref, m0, m1, m2, m3, tiles_ref, mixed_ref,
):
    me = me_ref[0]
    heads = table_ref.shape[1]
    tok = x0.shape[0]
    half = tok // 2
    pieces = ((x0, 0), (x1, tok), (x2a, 2 * tok), (x2b, 2 * tok + half), (x3a, 3 * tok), (x3b, 3 * tok + half))
    for ref, start in pieces:
        rows = ref.shape[0]
        projected = dot(ref[...], w_ref[...], 1, 1).astype(BF16)
        for which in range(3):
            for h in range(heads):
                at = (3 * h + which) * HEAD_DIM
                part = projected[:, at : at + HEAD_DIM]
                if which == 0:
                    part = part * jnp.asarray(0.125, BF16)
                proj_ref[which, h, start : start + rows, :] = part
    for h in range(heads):
        build_bias(table_ref, h, tiles_ref, tok)

        def block(j, carry):
            q = proj_ref[0, h, pl.ds(pl.multiple_of(j * tok, tok), tok), :]
            keys = proj_ref[1, h]
            seg_col = seg_col_ref[me ^ j]
            parts = masked_scores(me, j, q, keys, tiles_ref, seg_col, seg_row_ref, 4, tok)
            top = functools.reduce(jnp.maximum, parts)
            top = jnp.max(top, axis=1, keepdims=True)
            probs = [jnp.exp(s - top) for s in parts]
            total = jnp.sum(functools.reduce(jnp.add, probs), axis=1, keepdims=True)
            mixed = None
            for l in range(4):
                term = dot(probs[l].astype(BF16), proj_ref[2, h, l * tok : (l + 1) * tok, :])
                mixed = term if mixed is None else mixed + term
            mixed_ref[h, pl.ds(pl.multiple_of(j * tok, tok), tok), :] = (mixed / total).astype(BF16)
            lse_ref[h, pl.ds(pl.multiple_of(j * tok, tok), tok), :] = jnp.broadcast_to(
                top + jnp.log(total), (tok, 128)
            )
            return carry

        lax.fori_loop(0, 4, block, 0)
    for j, out in enumerate((m0, m1, m2, m3)):
        out[...] = jnp.concatenate(
            [mixed_ref[h, j * tok : (j + 1) * tok, :] for h in range(heads)], axis=1
        )


def backward_kernel(
    h, final, me_ref, table_ref, seg_row_ref, seg_col_ref, x0, x1, x2a, x2b, x3a, x3b, w_ref, gain_ref,
    proj_ref, lse_ref, g0, g1, g2, g3, *rest,
):
    me = me_ref[0]
    heads = table_ref.shape[1]
    tok = x0.shape[0]
    half = tok // 2
    if h:
        earlier, extra_before, *rest = rest
    dp_before, rest = (rest[: h - 1], rest[h - 1 :]) if final else ((), rest)
    if final:
        normed_grad_ref, *rest = rest
    else:
        dp_out, *rest = rest
    payload_ref, extra_ref, tiles_ref, sums_ref, do_ref, dkt_ref, dvt_ref, dp_ref, dpt_ref = rest
    width = HEAD_DIM
    for j, ref in enumerate((g0, g1, g2, g3)):
        do_ref[j * tok : (j + 1) * tok, :] = ref[:, h * width : (h + 1) * width]
    build_bias(table_ref, h, tiles_ref, tok)
    sums_ref[...] = jnp.zeros_like(sums_ref)
    dkt_ref[...] = jnp.zeros_like(dkt_ref)
    dvt_ref[...] = jnp.zeros_like(dvt_ref)

    def block(j, carry):
        rows = pl.ds(pl.multiple_of(j * tok, tok), tok)
        q = proj_ref[0, 0, rows, :]
        grad = do_ref[rows, :]
        seg_col = seg_col_ref[me ^ j]
        parts = masked_scores(me, j, q, proj_ref[1, 0], tiles_ref, seg_col, seg_row_ref, 4, tok)
        lse = lse_ref[0, rows, :][:, :1]
        probs, weighted = [], []
        for l in range(4):
            p = jnp.exp(parts[l] - lse)
            cut = slice(l * tok, (l + 1) * tok)
            dvt_ref[:, cut] += dot(grad, p.astype(BF16), 0, 0)
            probs.append(p)
            weighted.append(p * dot(grad, proj_ref[2, 0, cut, :], 1, 1))
        delta = jnp.sum(functools.reduce(jnp.add, weighted), axis=1, keepdims=True)
        dq = None
        for l in range(4):
            cut = slice(l * tok, (l + 1) * tok)
            ds = weighted[l] - probs[l] * delta
            at = tile_index(me, j, l)
            sums_ref[at] = sums_ref[at] + ds
            low = ds.astype(BF16)
            dkt_ref[:, cut] += dot(q, low, 0, 0)
            term = dot(low, proj_ref[1, 0, cut, :])
            dq = term if dq is None else dq + term
        dq = dq * 0.125
        dp_ref[rows, :width] = dq.astype(BF16)
        dpt_ref[j, :width, :] = dq.T.astype(BF16)
        return carry

    lax.fori_loop(0, 4, block, 0)
    dkt = dkt_ref[...]
    dvt = dvt_ref[...]
    dp_ref[:, width : 2 * width] = dkt.T.astype(BF16)
    dp_ref[:, 2 * width :] = dvt.T.astype(BF16)
    for j in range(4):
        cut = slice(j * tok, (j + 1) * tok)
        dpt_ref[j, width : 2 * width, :] = dkt[:, cut].astype(BF16)
        dpt_ref[j, 2 * width :, :] = dvt[:, cut].astype(BF16)

    strip = jnp.concatenate([sums_ref[1], sums_ref[2], sums_ref[3], jnp.zeros((tok, tok), F32)], axis=1)
    rows = tok
    while rows > 8:
        rows //= 2
        strip = strip[:rows] + pltpu.roll(strip[rows:], 4 * tok - rows, 1)
    diagonal = strip[0:1]
    for i in range(1, 8):
        diagonal = diagonal + pltpu.roll(strip[i : i + 1], 4 * tok - i, 1)
    col = lax.broadcasted_iota(jnp.int32, (1, 4 * tok), 1)
    bucket = bucket_of(col - tok - jnp.where(col >= 3 * tok, 4 * tok, 0))
    low_far = jnp.sum(jnp.sum(sums_ref[0], axis=0, keepdims=True), axis=1, keepdims=True)
    high_far = jnp.sum(jnp.sum(sums_ref[4], axis=0, keepdims=True), axis=1, keepdims=True)
    lane = lax.broadcasted_iota(jnp.int32, (1, D), 1) - me * (BUCKETS * heads)
    table_row = jnp.zeros((1, D), F32)
    for b in range(BUCKETS):
        value = jnp.sum(jnp.where(bucket == b, diagonal, 0.0), axis=1, keepdims=True)
        if b == 15:
            value = value + low_far
        if b == 31:
            value = value + high_far
        table_row = jnp.where(lane == b * heads + h, value, table_row)

    pieces = ((x0, 0, 0), (x1, 1, 0), (x2a, 2, 0), (x2b, 2, half), (x3a, 3, 0), (x3b, 3, half))
    total = None
    for ref, j, start in pieces:
        term = dot(dpt_ref[j, :, start : start + ref.shape[0]], ref[...])
        total = term if total is None else total + term
    payload_ref[...] = total.astype(BF16)
    gain_row = jnp.sum(total * w_ref[h].astype(F32), axis=0, keepdims=True) / gain_ref[...]
    row = lax.broadcasted_iota(jnp.int32, (8, D), 0)
    extra = jnp.where(row == 0, gain_row, jnp.where(row == 1, table_row, 0.0))
    extra_ref[...] = extra + extra_before[...] if h else extra
    if final:
        for j in range(4):
            cut = slice(j * tok, (j + 1) * tok)
            part = dot(dp_ref[cut, :], w_ref[h])
            for i, ref in enumerate((earlier, *dp_before)[: h]):
                part = part + dot(ref[cut, :], w_ref[i])
            normed_grad_ref[cut, :] = part.astype(BF16)
    else:
        dp_out[...] = dp_ref[...]


VMEM = pl.BlockSpec(memory_space=pltpu.VMEM)
SMEM = pl.BlockSpec(memory_space=pltpu.SMEM)
PARAMS = pltpu.CompilerParams(vmem_limit_bytes=48 * 1024 * 1024)


def halves(x, bit):
    n = x.shape[0] // 2
    upper = (lax.axis_index("expert") & bit) != 0
    keep = jnp.where(upper, x[n:], x[:n])
    send = jnp.where(upper, x[:n], x[n:])
    return keep, send


def add_low(a, b):
    return (a.astype(F32) + b.astype(F32)).astype(BF16)


def joined(x, other, bit):
    upper = (lax.axis_index("expert") & bit) != 0
    return jnp.concatenate([jnp.where(upper, other, x), jnp.where(upper, x, other)])


def shards(
    tokens,
    norm1_gain,
    qkv_weight,
    out_weight,
    bucket_position_bias,
    norm2_gain,
    router_weight,
    expert_in,
    expert_out,
    segment,
    route,
    slot,
    cotangent,
):
    highest_precision = lax.Precision.HIGHEST
    tok = tokens.shape[0]
    half = tok // 2
    seq = segment.shape[0]
    experts = router_weight.shape[1]
    capacity = (5 * tok + 4 * experts - 1) // (4 * experts)
    heads = bucket_position_bias.shape[1]
    width = out_weight.shape[0]
    me = lax.axis_index("shard").astype(jnp.int32).reshape(1)
    sources = lax.axis_size("expert")

    def over_x(v):
        return swap(v, "shard", 2)

    def over_core(v):
        return swap(v, "shard", 1)

    inputs = tokens.astype(F32)
    s1 = lax.rsqrt(jnp.mean(inputs * inputs, axis=-1, keepdims=True) + EPS)
    normed_low = (inputs * s1 * norm1_gain).astype(BF16)
    x2a = over_x(normed_low[:half])
    x2b = over_x(normed_low[half:])
    x1 = over_core(normed_low)
    x3a = over_core(x2a)
    x3b = over_core(x2b)
    pieces = (normed_low, x1, x2a, x2b, x3a, x3b)
    out_w1 = over_core(out_weight)
    out_w2 = over_x(after(out_weight, x2b))
    in_own, out_own = expert_in[0], expert_out[0]
    split_in, split_out = 5 * D // 8, D // 3
    in_far = over_x(in_own[:split_in])
    qkv_t = jnp.transpose(qkv_weight.reshape(3, D, heads, HEAD_DIM), (2, 0, 3, 1))
    qkv_t = qkv_t.reshape(heads, 3 * HEAD_DIM, D)
    seg_rows = segment.reshape(4, 1, tok)
    seg_cols = segment.reshape(4, tok, 1)

    sds = jax.ShapeDtypeStruct
    proj, lse, *mixed = pl.pallas_call(
        forward_kernel,
        out_shape=[sds((3, heads, seq, HEAD_DIM), BF16), sds((heads, seq, 128), F32)]
        + [sds((tok, width), BF16)] * 4,
        in_specs=[SMEM, SMEM] + [VMEM] * 9,
        out_specs=[VMEM] * 6,
        scratch_shapes=[pltpu.VMEM((5, tok, tok), F32), pltpu.VMEM((heads, seq, HEAD_DIM), BF16)],
        compiler_params=PARAMS,
        cost_estimate=pl.CostEstimate(flops=15 * 10**9, bytes_accessed=8 * 10**6, transcendentals=3 * 10**6),
        name="attention_forward",
    )(me, bucket_position_bias, seg_rows, seg_cols, *pieces, qkv_t.reshape(3 * width, D))

    *mixed, in_far, out_w2 = lax.optimization_barrier((*mixed, in_far, out_w2))
    out_w3 = over_core(out_w2)
    out_w = jnp.concatenate([out_weight, out_w1, out_w2, out_w3])
    in_rest = over_x(after(in_own[split_in:], in_far))
    out_far = over_x(after(out_own[:split_out], in_far))
    out_rest = over_x(after(out_own[split_out:], out_far))
    mixed_own = jnp.concatenate(
        [mixed[0]] + [swap(mixed[k], "shard", k) for k in (1, 2, 3)], axis=1
    )
    attended = dot(mixed_own, out_w)
    hidden = inputs + attended
    s2 = lax.rsqrt(jnp.mean(hidden * hidden, axis=-1, keepdims=True) + EPS)
    routed_low = (hidden * s2 * norm2_gain).astype(BF16)
    routed_full = routed_low.astype(F32)
    chosen = (route[:, None] == jnp.arange(experts, dtype=jnp.int32)[None, :]).astype(F32)
    router_probs = jax.nn.softmax(jnp.dot(routed_full, router_weight, precision=highest_precision), axis=-1)
    gate = jnp.sum(router_probs * chosen, axis=-1, keepdims=True)
    upstream = cotangent.astype(F32)

    columns = jnp.arange(experts * capacity, dtype=jnp.int32)
    if sources == 8:
        order = columns // capacity ^ (lax.axis_index("expert") * (experts // sources))
        columns = order * capacity + columns % capacity
    placed = ((route * capacity + slot)[:, None] == columns[None, :]) & (slot[:, None] >= 0)
    dispatch = placed.astype(BF16)
    both = jnp.concatenate([routed_low, (gate * upstream).astype(BF16)], axis=1)
    outgoing = dot(dispatch, both, 0, 0).astype(BF16)
    arrived = exchange(outgoing, (in_rest, out_far))
    arrived, out_rest = lax.optimization_barrier((arrived, out_rest))
    in_far = jnp.concatenate([in_far, in_rest])
    out_far = jnp.concatenate([out_far, out_rest])
    beside = over_core(arrived)
    rows = jnp.concatenate([arrived[:, :D], beside[:, :D]])
    grads = jnp.concatenate([arrived[:, D:], beside[:, D:]])
    count = experts * capacity

    def expert_half(w_in, w_out):
        upward = dot(rows, w_in)
        active, gelu_back = jax.vjp(gelu_tanh, upward)
        active = active.astype(BF16)
        active_grad = dot(grads, w_out, 1, 1)
        upward_grad = gelu_back(active_grad)[0].astype(BF16)
        return active, upward_grad

    active_far, upward_far = expert_half(in_far, out_far)
    in_grad_far = over_x(dot(rows, upward_far, 0, 0).astype(BF16))
    out_grad_far = dot(active_far, grads, 0, 0).astype(BF16)
    active_own, upward_own = expert_half(in_own, out_own)
    produced = dot(active_own, out_own) + dot(active_far, out_far)
    row_grad = dot(upward_own, in_own, 1, 1) + dot(upward_far, in_far, 1, 1)
    mine = jnp.concatenate([produced[:count], row_grad[:count]], axis=1)
    theirs = jnp.concatenate([produced[count:], row_grad[count:]], axis=1).astype(BF16)
    returned = exchange(add_low(mine, over_core(theirs)))
    returned, in_grad_far = lax.optimization_barrier((returned, in_grad_far))
    in_grad_own = dot(rows, upward_own, 0, 0)
    out_grad_own = dot(active_own, grads, 0, 0)
    back = dot(dispatch, returned)
    combined, expert_grad = back[:, :D], back[:, D:]
    output = (hidden + gate * combined).astype(BF16)
    gate_grad = jnp.sum(upstream * combined, axis=-1, keepdims=True)
    logit_grad = router_probs * (gate_grad * chosen - gate_grad * gate)
    router_grad = lax.dot_general(
        logit_grad, routed_full, (((0,), (0,)), ((), ())), precision=highest_precision
    )
    routed_grad = expert_grad + lax.dot_general(
        logit_grad, router_weight, (((1,), (1,)), ((), ())), precision=highest_precision
    )
    norm2_grad = jnp.sum(routed_grad * hidden * s2, axis=0, keepdims=True)
    scaled = routed_grad * norm2_gain
    hidden_grad = (
        upstream + s2 * scaled - hidden * s2**3 * jnp.mean(scaled * hidden, axis=-1, keepdims=True)
    )
    branch_low = hidden_grad.astype(BF16)
    mixed_grad = dot(branch_low, out_w, 1, 1).astype(BF16)
    mixed_grads = [mixed_grad[:, :width]] + [
        swap(mixed_grad[:, k * width : (k + 1) * width], "shard", k) for k in (1, 2, 3)
    ]
    branch1 = over_core(branch_low)
    branch2 = over_x(after(branch_low, mixed_grads[2], mixed_grads[3]))
    def head_gradients(h, grads, earlier):
        final = h == heads - 1
        one = pl.BlockSpec((3, 1, seq, HEAD_DIM), lambda i: (0, h, 0, 0))
        log = pl.BlockSpec((1, seq, 128), lambda i: (h, 0, 0))
        return pl.pallas_call(
            functools.partial(backward_kernel, h, final),
            grid=(1,),
            out_shape=[
                sds((seq, D), BF16) if final else sds((seq, 3 * HEAD_DIM), BF16),
                sds((3 * HEAD_DIM, D), BF16),
                sds((8, D), F32),
            ],
            in_specs=[SMEM, SMEM] + [VMEM] * 10 + [one, log] + [VMEM] * (4 + len(earlier)),
            out_specs=[VMEM] * 3,
            scratch_shapes=[
                pltpu.VMEM((5, tok, tok), F32),
                pltpu.VMEM((5, tok, tok), F32),
                pltpu.VMEM((seq, HEAD_DIM), BF16),
                pltpu.VMEM((HEAD_DIM, seq), F32),
                pltpu.VMEM((HEAD_DIM, seq), F32),
                pltpu.VMEM((seq, 3 * HEAD_DIM), BF16),
                pltpu.VMEM((4, 3 * HEAD_DIM, tok), BF16),
            ],
            compiler_params=PARAMS,
            cost_estimate=pl.CostEstimate(flops=8 * 10**9, bytes_accessed=6 * 10**6, transcendentals=10**6),
            name="attention_backward_%d" % h,
        )(
            me, bucket_position_bias, seg_rows, seg_cols, *pieces, qkv_t, norm1_gain.reshape(1, D),
            proj, lse, *grads, *earlier,
        )

    dps, payloads, extra = [], [], None
    for h in range(heads):
        if h == 1:
            mixed_grads[0], branch2 = lax.optimization_barrier((mixed_grads[0], branch2))
        earlier = []
        if h:
            earlier = [dps[0], extra]
        if h == heads - 1:
            earlier += dps[1:]
        dp, payload, extra = head_gradients(h, mixed_grads, earlier)
        dps.append(dp)
        payloads.append(payload)
    normed_part = dps[-1]
    branch3 = over_core(branch2)
    out_grad = sum(dot(mixed[k], b, 0, 0) for k, b in enumerate((branch_low, branch1, branch2, branch3)))
    small = jnp.concatenate([norm2_grad, router_grad])
    small = jnp.concatenate([small, extra[:2]])
    wide = [
        jnp.concatenate(payloads[1:]),
        jnp.concatenate([payloads[0], out_grad.astype(BF16)]),
    ]
    in_step = sources == 8
    bits = ((1, 2), (2, 1))
    pair = normed_part.reshape(2, 2, tok, D)
    small_other, normed_other = over_core(small), over_core(pair[:, 1])
    out_grad_far = over_x(after(out_grad_far, branch2))
    if in_step:
        cuts = [halves(part, bit[0]) for part, bit in zip(wide, bits)]
        got = [swap(send, "expert", bit[0]) for (_, send), bit in zip(cuts, bits)]
        *got, small_other, normed_other, out_grad_far = lax.optimization_barrier(
            (*got, small_other, normed_other, out_grad_far)
        )
        wide = [add_low(keep, other) for (keep, _), other in zip(cuts, got)]
    small = small + small_other
    near = pair[:, 0].astype(F32) + normed_other.astype(F32)
    small_other, normed_other = over_x(small), over_x(near[1].astype(BF16))
    expert_in_grad = (in_grad_own + in_grad_far.astype(F32))[None]
    if in_step:
        cuts = [halves(part, bit[1]) for part, bit in zip(wide, bits)]
        got = [swap(send, "expert", bit[1]) for (_, send), bit in zip(cuts, bits)]
        *got, small_other, normed_other, expert_in_grad = lax.optimization_barrier(
            (*got, small_other, normed_other, expert_in_grad)
        )
        wide = [add_low(keep, other) for (keep, _), other in zip(cuts, got)]
    small = small + small_other
    normed_grad = near[0] + normed_other.astype(F32)
    scaled1 = normed_grad * norm1_gain
    input_grad = (
        hidden_grad
        + s1 * scaled1
        - inputs * s1**3 * jnp.mean(scaled1 * inputs, axis=-1, keepdims=True)
    )
    expert_out_grad = (out_grad_own + out_grad_far.astype(F32))[None]
    if in_step:
        got = [swap(part, "expert", 4) for part in wide]
        small_other = swap(small, "expert", 1)
        *got, small_other, input_grad, expert_out_grad = lax.optimization_barrier(
            (*got, small_other, input_grad, expert_out_grad)
        )
        wide = [add_low(part, other) for part, other in zip(wide, got)]
        small = small + small_other
        for step, bit_small in ((1, 2), (0, 4)):
            got = [swap(part, "expert", bit[step]) for part, bit in zip(wide, bits)]
            small_other = swap(small, "expert", bit_small)
            *got, small_other = lax.optimization_barrier((*got, small_other))
            wide = [joined(part, other, bit[step]) for part, other, bit in zip(wide, got, bits)]
            small = small + small_other
        one, two = wide
    else:
        one, two, small = lax.psum((wide[0].astype(F32), wide[1].astype(F32), small), "expert")
    qkv_grad = jnp.concatenate([two[: 3 * HEAD_DIM], one])
    qkv_grad = jnp.transpose(qkv_grad.reshape(heads, 3, HEAD_DIM, D), (1, 3, 0, 2))
    qkv_grad = qkv_grad.reshape(3, D, width).astype(F32)
    norm1_grad = small[experts + 1]
    table_size = BUCKETS * heads
    table_grad = lax.dynamic_slice_in_dim(small[experts + 2], me[0] * table_size, table_size)
    table_grad = table_grad.reshape(BUCKETS, heads)
    return (
        output,
        input_grad,
        norm1_grad,
        qkv_grad,
        two[3 * HEAD_DIM :].astype(F32),
        table_grad,
        small[0],
        jnp.transpose(small[1 : experts + 1]),
        expert_in_grad,
        expert_out_grad,
    )


def solution(mesh):
    placed = (
        P(("expert", "shard"), None),
        P(),
        P(None, None, "shard"),
        P("shard", None),
        P(None, "shard"),
        P(),
        P(),
        P("expert", None, "shard"),
        P("expert", "shard", None),
        P("expert"),
        P(("expert", "shard")),
        P(("expert", "shard")),
        P(("expert", "shard"), None),
    )
    return jax.shard_map(
        shards,
        mesh=mesh,
        in_specs=placed,
        out_specs=(
            P(("expert", "shard"), None),
            P(("expert", "shard"), None),
            P(),
            P(None, None, "shard"),
            P("shard", None),
            P(None, "shard"),
            P(),
            P(),
            P("expert", None, "shard"),
            P("expert", "shard", None),
        ),
        check_vma=False,
    )
```

```python
import functools

import jax
import jax.numpy as jnp
from jax import lax
from jax.experimental import pallas as pl
from jax.experimental.pallas import tpu as pltpu
from jax.sharding import PartitionSpec as P

D = 768
HEAD_DIM = 64
BUCKETS = 32


EPS = 1e-06
THRESHOLDS = (12, 16, 23, 32, 46, 64, 91)
NEG = -1000000000.0
F32 = jnp.float32
ORDER = (6, 7, 4, 2, 3, 1, 5, 0)
BF16 = jnp.bfloat16


def bucket_of(relative):
    distance = jnp.abs(relative)
    far = 8 + sum(((distance >= edge).astype(jnp.int32) for edge in THRESHOLDS))
    near = jnp.where(distance < 8, distance, jnp.minimum(far, 15))
    return near + jnp.where(relative > 0, 16, 0)


def rms_norm(values, gain):
    return values * lax.rsqrt(jnp.mean(values * values, axis=-1, keepdims=True) + EPS) * gain


def gelu_tanh(values):
    return jax.nn.gelu(values, approximate=True)


def dot(a, b, ca=1, cb=0):
    return lax.dot_general(a, b, (((ca,), (cb,)), ((), ())), preferred_element_type=F32)


def swap(x, axis, bit):
    size = lax.axis_size(axis)
    return lax.ppermute(x, axis, [(i, i ^ bit) for i in range(size)])


def after(x, *others):
    return lax.optimization_barrier((x, *others))[0]


def exchange(rows):
    size = lax.axis_size("expert")
    count = rows.shape[0] // size
    if size != 8:
        return lax.all_to_all(rows, "expert", split_axis=0, concat_axis=0, tiled=True)
    blocks = [rows[k * count : (k + 1) * count] for k in range(size)]
    blocks = [swap(x, "expert", k) if k else x for k, x in zip(ORDER, blocks)]
    return jnp.concatenate(blocks)


def build_bias(table_ref, head, tiles_ref, tok):
    wide = 4 * tok
    row = lax.broadcasted_iota(jnp.int32, (8, wide), 0)
    col = lax.broadcasted_iota(jnp.int32, (8, wide), 1)
    relative = col - tok - row - jnp.where(col >= 3 * tok, wide, 0)
    bucket = bucket_of(relative)
    base = jnp.zeros((8, wide), F32)
    for b in range(BUCKETS):
        base = jnp.where(bucket == b, table_ref[b, head], base)
    for a in range(tok // 8):
        rows = pltpu.roll(base, 8 * a, 1) if a else base
        for d in range(3):
            tiles_ref[d + 1, 8 * a : 8 * a + 8, :] = rows[:, d * tok : (d + 1) * tok]
    tiles_ref[0] = jnp.full((tok, tok), table_ref[15, head], F32)
    tiles_ref[4] = jnp.full((tok, tok), table_ref[31, head], F32)


def tile_index(me, j, l):
    return jnp.clip((me ^ l) - (me ^ j), -2, 2) + 2


def masked_scores(me, j, q, keys, tiles_ref, seg_col, seg_row_ref, blocks, tok):
    parts = []
    for l in range(blocks):
        s = dot(q, keys[:, l * tok : (l + 1) * tok])
        s = s + tiles_ref[tile_index(me, j, l)]
        parts.append(jnp.where(seg_col == seg_row_ref[me ^ l], s, NEG))
    return parts


def forward_kernel(
    me_ref, table_ref, seg_row_ref, seg_col_ref, x0, x1, x2a, x2b, x3a, x3b, w_ref,
    proj_ref, lse_ref, m0, m1, m2, m3, tiles_ref, mixed_ref, kt_ref,
):
    me = me_ref[0]
    heads = table_ref.shape[1]
    tok = x0.shape[0]
    half = tok // 2
    pieces = ((x0, 0), (x1, tok), (x2a, 2 * tok), (x2b, 2 * tok + half), (x3a, 3 * tok), (x3b, 3 * tok + half))
    for ref, start in pieces:
        rows = ref.shape[0]
        projected = dot(ref[...], w_ref[...], 1, 1).astype(BF16)
        for which in range(3):
            for h in range(heads):
                at = (3 * h + which) * HEAD_DIM
                part = projected[:, at : at + HEAD_DIM]
                if which == 0:
                    part = part * jnp.asarray(0.125, BF16)
                proj_ref[which, h, start : start + rows, :] = part
    for h in range(heads):
        build_bias(table_ref, h, tiles_ref, tok)

        kt_ref[...] = proj_ref[1, h].astype(F32).T.astype(BF16)

        def block(j, carry):
            q = proj_ref[0, h, pl.ds(pl.multiple_of(j * tok, tok), tok), :]
            keys = kt_ref[...]
            seg_col = seg_col_ref[me ^ j]
            parts = masked_scores(me, j, q, keys, tiles_ref, seg_col, seg_row_ref, 4, tok)
            top = functools.reduce(jnp.maximum, parts)
            top = jnp.max(top, axis=1, keepdims=True)
            probs = [jnp.exp(s - top) for s in parts]
            total = jnp.sum(functools.reduce(jnp.add, probs), axis=1, keepdims=True)
            mixed = None
            for l in range(4):
                term = dot(probs[l].astype(BF16), proj_ref[2, h, l * tok : (l + 1) * tok, :])
                mixed = term if mixed is None else mixed + term
            mixed_ref[h, pl.ds(pl.multiple_of(j * tok, tok), tok), :] = (mixed / total).astype(BF16)
            lse_ref[h, pl.ds(pl.multiple_of(j * tok, tok), tok), :] = jnp.broadcast_to(
                top + jnp.log(total), (tok, 128)
            )
            return carry

        lax.fori_loop(0, 4, block, 0, unroll=4)
    for j, out in enumerate((m0, m1, m2, m3)):
        out[...] = jnp.concatenate(
            [mixed_ref[h, j * tok : (j + 1) * tok, :] for h in range(heads)], axis=1
        )


def backward_kernel(
    h, final, me_ref, table_ref, seg_row_ref, seg_col_ref, x0, x1, x2a, x2b, x3a, x3b, w_ref, gain_ref,
    proj_ref, lse_ref, g0, g1, g2, g3, *rest,
):
    me = me_ref[0]
    heads = table_ref.shape[1]
    tok = x0.shape[0]
    half = tok // 2
    if h:
        earlier, extra_before, *rest = rest
    dp_before, rest = (rest[: h - 1], rest[h - 1 :]) if final else ((), rest)
    if final:
        normed_near_ref, normed_send_ref, *rest = rest
    else:
        dp_out, *rest = rest
    payload_ref, extra_ref, tiles_ref, sums_ref, do_ref, dkt_ref, dvt_ref, dp_ref, dpt_ref, kt_ref, vt_ref = rest
    width = HEAD_DIM
    for j, ref in enumerate((g0, g1, g2, g3)):
        do_ref[j * tok : (j + 1) * tok, :] = ref[:, h * width : (h + 1) * width]
    build_bias(table_ref, h, tiles_ref, tok)
    sums_ref[...] = jnp.zeros_like(sums_ref)
    dkt_ref[...] = jnp.zeros_like(dkt_ref)
    dvt_ref[...] = jnp.zeros_like(dvt_ref)

    kt_ref[...] = proj_ref[1, 0].astype(F32).T.astype(BF16)
    vt_ref[...] = proj_ref[2, 0].astype(F32).T.astype(BF16)

    def block(j, carry):
        rows = pl.ds(pl.multiple_of(j * tok, tok), tok)
        q = proj_ref[0, 0, rows, :]
        grad = do_ref[rows, :]
        q_t = q.astype(F32).T.astype(BF16)
        grad_t = grad.astype(F32).T.astype(BF16)
        seg_col = seg_col_ref[me ^ j]
        parts = masked_scores(me, j, q, kt_ref[...], tiles_ref, seg_col, seg_row_ref, 4, tok)
        lse = lse_ref[0, rows, :][:, :1]
        probs, weighted = [], []
        for l in range(4):
            p = jnp.exp(parts[l] - lse)
            cut = slice(l * tok, (l + 1) * tok)
            dvt_ref[:, cut] += dot(grad_t, p.astype(BF16))
            probs.append(p)
            weighted.append(p * dot(grad, vt_ref[:, cut]))
        delta = jnp.sum(functools.reduce(jnp.add, weighted), axis=1, keepdims=True)
        dq = None
        for l in range(4):
            cut = slice(l * tok, (l + 1) * tok)
            ds = weighted[l] - probs[l] * delta
            at = tile_index(me, j, l)
            sums_ref[at] = sums_ref[at] + ds
            low = ds.astype(BF16)
            dkt_ref[:, cut] += dot(q_t, low)
            term = dot(low, proj_ref[1, 0, cut, :])
            dq = term if dq is None else dq + term
        dq = dq * 0.125
        dp_ref[rows, :width] = dq.astype(BF16)
        dpt_ref[j, :width, :] = dq.T.astype(BF16)
        return carry

    lax.fori_loop(0, 4, block, 0, unroll=4)
    dkt = dkt_ref[...]
    dvt = dvt_ref[...]
    dp_ref[:, width : 2 * width] = dkt.T.astype(BF16)
    dp_ref[:, 2 * width :] = dvt.T.astype(BF16)
    for j in range(4):
        cut = slice(j * tok, (j + 1) * tok)
        dpt_ref[j, width : 2 * width, :] = dkt[:, cut].astype(BF16)
        dpt_ref[j, 2 * width :, :] = dvt[:, cut].astype(BF16)

    strip = jnp.concatenate([sums_ref[1], sums_ref[2], sums_ref[3], jnp.zeros((tok, tok), F32)], axis=1)
    rows = tok
    while rows > 8:
        rows //= 2
        strip = strip[:rows] + pltpu.roll(strip[rows:], 4 * tok - rows, 1)
    diagonal = strip[0:1]
    for i in range(1, 8):
        diagonal = diagonal + pltpu.roll(strip[i : i + 1], 4 * tok - i, 1)
    col = lax.broadcasted_iota(jnp.int32, (1, 4 * tok), 1)
    bucket = bucket_of(col - tok - jnp.where(col >= 3 * tok, 4 * tok, 0))
    low_far = jnp.sum(jnp.sum(sums_ref[0], axis=0, keepdims=True), axis=1, keepdims=True)
    high_far = jnp.sum(jnp.sum(sums_ref[4], axis=0, keepdims=True), axis=1, keepdims=True)
    entry = lax.broadcasted_iota(jnp.int32, (BUCKETS, 1), 0)
    values = jnp.sum(jnp.where(bucket == entry, diagonal, 0.0), axis=1, keepdims=True)
    values = values + jnp.where(entry == 15, low_far, 0.0) + jnp.where(entry == 31, high_far, 0.0)
    lane = lax.broadcasted_iota(jnp.int32, (BUCKETS, D), 1) - me * (BUCKETS * heads)
    at = lax.broadcasted_iota(jnp.int32, (BUCKETS, D), 0) * heads + h
    table_row = jnp.sum(jnp.where(lane == at, values, 0.0), axis=0, keepdims=True)

    pieces = ((x0, 0, 0), (x1, 1, 0), (x2a, 2, 0), (x2b, 2, half), (x3a, 3, 0), (x3b, 3, half))
    total = None
    for ref, j, start in pieces:
        term = dot(dpt_ref[j, :, start : start + ref.shape[0]], ref[...])
        total = term if total is None else total + term
    payload_ref[...] = total.astype(BF16)
    gain_row = jnp.sum(total * w_ref[h].astype(F32), axis=0, keepdims=True) / gain_ref[...]
    row = lax.broadcasted_iota(jnp.int32, (8, D), 0)
    extra = jnp.where(row == 0, gain_row, jnp.where(row == 1, table_row, 0.0))
    extra_ref[...] = extra + extra_before[...] if h else extra
    if final:
        for j in range(4):
            cut = slice(j * tok, (j + 1) * tok)
            part = dot(dp_ref[cut, :], w_ref[h])
            for i, ref in enumerate((earlier, *dp_before)[: h]):
                part = part + dot(ref[cut, :], w_ref[i])
            if j % 2:
                normed_send_ref[j // 2] = part.astype(BF16)
            else:
                normed_near_ref[j // 2] = part
    else:
        dp_out[...] = dp_ref[...]


def expert_kernel(
    near_ref, beside_ref, far_a, far_b, far_c, out_far, in_own, out_own,
    active_own, upward_own, rows_ref, grads_ref, in_grad_far, out_grad_far, mine_ref, theirs_ref,
    active_far, upward_far, in_far,
):
    count = near_ref.shape[0]
    rows_ref[:count, :] = near_ref[:, :D]
    rows_ref[count:, :] = beside_ref[:, :D]
    grads_ref[:count, :] = near_ref[:, D:]
    grads_ref[count:, :] = beside_ref[:, D:]
    at = 0
    for ref in (far_a, far_b, far_c):
        in_far[at : at + ref.shape[0], :] = ref[...]
        at += ref.shape[0]
    wide = 256
    c0, c1 = 0.7978845608028654, 0.044715
    for w_in, w_out, active_ref, upward_ref in (
        (in_own, out_own, active_own, upward_own),
        (in_far, out_far, active_far, upward_far),
    ):
        for at in range(0, w_in.shape[1], wide):
            cut = slice(at, at + wide)
            for r in range(0, 2 * count, count):
                part = slice(r, r + count)
                v = dot(rows_ref[part, :], w_in[:, cut])
                square = v * v
                t = jnp.tanh(c0 * (v + c1 * (square * v)))
                half = 0.5 + 0.5 * t
                active_ref[part, cut] = (v * half).astype(BF16)
                slope = half + (0.5 * c0) * v * (1.0 - t * t) * (1.0 + (3.0 * c1) * square)
                grad = dot(grads_ref[part, :], w_out[cut, :], 1, 1)
                upward_ref[part, cut] = (grad * slope).astype(BF16)
    for at in range(0, D, wide):
        cut = slice(at, at + wide)
        into = slice(D + at, D + at + wide)
        for r in (count, 0):
            part = slice(r, r + count)
            produced = dot(active_own[part, :], out_own[:, cut]) + dot(active_far[part, :], out_far[:, cut])
            row_grad = dot(upward_own[part, :], in_own[cut, :], 1, 1) + dot(
                upward_far[part, :], in_far[cut, :], 1, 1
            )
            if r:
                theirs_ref[:, cut] = produced.astype(BF16)
                theirs_ref[:, into] = row_grad.astype(BF16)
            else:
                mine_ref[:, cut] = produced
                mine_ref[:, into] = row_grad
        in_grad_far[:, cut] = dot(rows_ref[...], upward_far[:, cut], 0, 0).astype(BF16)
        out_grad_far[:, cut] = dot(active_far[...], grads_ref[:, cut], 0, 0).astype(BF16)


VMEM = pl.BlockSpec(memory_space=pltpu.VMEM)
SMEM = pl.BlockSpec(memory_space=pltpu.SMEM)
PARAMS = pltpu.CompilerParams(vmem_limit_bytes=24 * 1024 * 1024)


def halves(x, bit):
    n = x.shape[0] // 2
    upper = (lax.axis_index("expert") & bit) != 0
    keep = jnp.where(upper, x[n:], x[:n])
    send = jnp.where(upper, x[:n], x[n:])
    return keep, send


def add_low(a, b):
    return (a.astype(F32) + b.astype(F32)).astype(BF16)


def joined(x, other, bit):
    upper = (lax.axis_index("expert") & bit) != 0
    return jnp.concatenate([jnp.where(upper, other, x), jnp.where(upper, x, other)])


def shards(
    tokens,
    norm1_gain,
    qkv_weight,
    out_weight,
    bucket_position_bias,
    norm2_gain,
    router_weight,
    expert_in,
    expert_out,
    segment,
    route,
    slot,
    cotangent,
):
    highest_precision = lax.Precision.HIGHEST
    tok = tokens.shape[0]
    half = tok // 2
    seq = segment.shape[0]
    experts = router_weight.shape[1]
    capacity = (5 * tok + 4 * experts - 1) // (4 * experts)
    heads = bucket_position_bias.shape[1]
    width = out_weight.shape[0]
    me = lax.axis_index("shard").astype(jnp.int32).reshape(1)
    sources = lax.axis_size("expert")

    def over_x(v):
        return swap(v, "shard", 2)

    def over_core(v):
        return swap(v, "shard", 1)

    inputs = tokens.astype(F32)
    s1 = lax.rsqrt(jnp.mean(inputs * inputs, axis=-1, keepdims=True) + EPS)
    normed_low = (inputs * s1 * norm1_gain).astype(BF16)
    x2a = over_x(normed_low[:half])
    x2b = over_x(normed_low[half:])
    x1 = over_core(normed_low)
    x3a = over_core(x2a)
    x3b = over_core(x2b)
    pieces = (normed_low, x1, x2a, x2b, x3a, x3b)
    out_w1 = over_core(out_weight)
    out_w2 = over_x(out_weight)
    in_own, out_own = expert_in[0], expert_out[0]
    split = 13 * D // 24
    split_again = 3 * D // 4
    in_far = over_x(after(in_own[:split], x2b))
    qkv_t = jnp.transpose(qkv_weight.reshape(3, D, heads, HEAD_DIM), (2, 0, 3, 1))
    qkv_t = qkv_t.reshape(heads, 3 * HEAD_DIM, D)
    seg_rows = segment.reshape(4, 1, tok)
    seg_cols = segment.reshape(4, tok, 1)

    sds = jax.ShapeDtypeStruct
    proj, lse, *mixed = pl.pallas_call(
        forward_kernel,
        out_shape=[sds((3, heads, seq, HEAD_DIM), BF16), sds((heads, seq, 128), F32)]
        + [sds((tok, width), BF16)] * 4,
        in_specs=[SMEM, SMEM] + [VMEM] * 9,
        out_specs=[VMEM] * 6,
        scratch_shapes=[
            pltpu.VMEM((5, tok, tok), F32),
            pltpu.VMEM((heads, seq, HEAD_DIM), BF16),
            pltpu.VMEM((HEAD_DIM, seq), BF16),
        ],
        compiler_params=PARAMS,
        cost_estimate=pl.CostEstimate(flops=15 * 10**9, bytes_accessed=8 * 10**6, transcendentals=3 * 10**6),
        name="attention_forward",
    )(me, bucket_position_bias, seg_rows, seg_cols, *pieces, qkv_t.reshape(3 * width, D))

    *mixed, out_w2, in_far = lax.optimization_barrier((*mixed, out_w2, in_far))
    out_w3 = over_core(out_w2)
    out_w = jnp.concatenate([out_weight, out_w1, out_w2, out_w3])
    mixed_in = [swap(mixed[k], "shard", k) for k in (1, 2, 3)]
    in_rest = over_x(after(in_own[split:split_again], mixed_in[0]))
    in_last = over_x(after(in_own[split_again:], mixed_in[0]))
    out_far = over_x(after(out_own, mixed_in[0]))
    mixed_own = jnp.concatenate([mixed[0]] + mixed_in, axis=1)
    attended = dot(mixed_own, out_w)
    hidden = inputs + attended
    s2 = lax.rsqrt(jnp.mean(hidden * hidden, axis=-1, keepdims=True) + EPS)
    routed_low = (hidden * s2 * norm2_gain).astype(BF16)
    routed_full = routed_low.astype(F32)
    chosen = (route[:, None] == jnp.arange(experts, dtype=jnp.int32)[None, :]).astype(F32)
    router_probs = jax.nn.softmax(jnp.dot(routed_full, router_weight, precision=highest_precision), axis=-1)
    gate = jnp.sum(router_probs * chosen, axis=-1, keepdims=True)
    upstream = cotangent.astype(F32)

    columns = jnp.arange(experts * capacity, dtype=jnp.int32)
    if sources == 8 == experts:
        order = jnp.repeat(jnp.asarray(ORDER, jnp.int32), capacity) ^ lax.axis_index("expert")
        columns = order * capacity + columns % capacity
    placed = ((route * capacity + slot)[:, None] == columns[None, :]) & (slot[:, None] >= 0)
    dispatch = placed.astype(BF16)
    both = jnp.concatenate([routed_low, (gate * upstream).astype(BF16)], axis=1)
    outgoing = dot(dispatch, both, 0, 0).astype(BF16)
    outgoing, in_rest = lax.optimization_barrier((outgoing, in_rest))
    arrived = exchange(outgoing)
    in_last, out_far, arrived = lax.optimization_barrier((in_last, out_far, arrived))
    beside = over_core(arrived)
    count = experts * capacity

    active_own, upward_own, rows, grads, in_grad_far, out_grad_far, mine, theirs = pl.pallas_call(
        expert_kernel,
        out_shape=[sds((2 * count, D), BF16)] * 4 + [sds((D, D), BF16)] * 2 + [sds((count, 2 * D), F32), sds((count, 2 * D), BF16)],
        in_specs=[VMEM] * 8,
        out_specs=[VMEM] * 8,
        scratch_shapes=[pltpu.VMEM((2 * count, D), BF16)] * 2 + [pltpu.VMEM((D, D), BF16)],
        compiler_params=PARAMS,
        cost_estimate=pl.CostEstimate(flops=8 * 10**9, bytes_accessed=12 * 10**6, transcendentals=10**6),
        name="experts",
    )(arrived, beside, in_far, in_rest, in_last, out_far, in_own, out_own)
    in_grad_far = over_x(in_grad_far)
    returned = exchange(add_low(mine, over_core(theirs)))
    returned, in_grad_far = lax.optimization_barrier((returned, in_grad_far))
    back = dot(dispatch, returned)
    combined, expert_grad = back[:, :D], back[:, D:]
    output = (hidden + gate * combined).astype(BF16)
    gate_grad = jnp.sum(upstream * combined, axis=-1, keepdims=True)
    logit_grad = router_probs * (gate_grad * chosen - gate_grad * gate)
    router_grad = lax.dot_general(
        logit_grad, routed_full, (((0,), (0,)), ((), ())), precision=highest_precision
    )
    routed_grad = expert_grad + lax.dot_general(
        logit_grad, router_weight, (((1,), (1,)), ((), ())), precision=highest_precision
    )
    norm2_grad = jnp.sum(routed_grad * hidden * s2, axis=0, keepdims=True)
    scaled = routed_grad * norm2_gain
    hidden_grad = (
        upstream + s2 * scaled - hidden * s2**3 * jnp.mean(scaled * hidden, axis=-1, keepdims=True)
    )
    branch_low = hidden_grad.astype(BF16)
    mixed_grad = dot(branch_low, out_w, 1, 1).astype(BF16)
    mixed_grads = [mixed_grad[:, :width]] + [
        swap(mixed_grad[:, k * width : (k + 1) * width], "shard", k) for k in (1, 2, 3)
    ]
    branch1 = over_core(branch_low)
    branch2 = over_x(after(branch_low, mixed_grads[1]))
    def head_gradients(h, grads, earlier):
        final = h == heads - 1
        one = pl.BlockSpec((3, 1, seq, HEAD_DIM), lambda i: (0, h, 0, 0))
        log = pl.BlockSpec((1, seq, 128), lambda i: (h, 0, 0))
        return pl.pallas_call(
            functools.partial(backward_kernel, h, final),
            grid=(1,),
            out_shape=[sds((2, tok, D), F32), sds((2, tok, D), BF16)] * final
            + [sds((seq, 3 * HEAD_DIM), BF16)] * (not final)
            + [
                sds((3 * HEAD_DIM, D), BF16),
                sds((8, D), F32),
            ],
            in_specs=[SMEM, SMEM] + [VMEM] * 10 + [one, log] + [VMEM] * (4 + len(earlier)),
            out_specs=[VMEM] * (3 + final),
            scratch_shapes=[
                pltpu.VMEM((5, tok, tok), F32),
                pltpu.VMEM((5, tok, tok), F32),
                pltpu.VMEM((seq, HEAD_DIM), BF16),
                pltpu.VMEM((HEAD_DIM, seq), F32),
                pltpu.VMEM((HEAD_DIM, seq), F32),
                pltpu.VMEM((seq, 3 * HEAD_DIM), BF16),
                pltpu.VMEM((4, 3 * HEAD_DIM, tok), BF16),
                pltpu.VMEM((HEAD_DIM, seq), BF16),
                pltpu.VMEM((HEAD_DIM, seq), BF16),
            ],
            compiler_params=PARAMS,
            cost_estimate=pl.CostEstimate(flops=8 * 10**9, bytes_accessed=6 * 10**6, transcendentals=10**6),
            name="attention_backward_%d" % h,
        )(
            me, bucket_position_bias, seg_rows, seg_cols, *pieces, qkv_t, norm1_gain.reshape(1, D),
            proj, lse, *grads, *earlier,
        )

    in_step = sources == 8

    def scatter(part, bit):
        keep, send = halves(part, bit)
        return keep, swap(send, "expert", bit)

    dps, payloads, extra = [], [], None
    for h in range(heads):
        if h == 1:
            mixed_grads[0], branch2 = lax.optimization_barrier((mixed_grads[0], branch2))
            branch3 = over_core(branch2)
            branches = (branch_low, branch1, branch2, branch3)
            out_grad = sum(dot(mixed[k], b, 0, 0) for k, b in enumerate(branches))
            ahead = jnp.concatenate([payloads[0], out_grad.astype(BF16)])
            if in_step:
                keep, other = scatter(ahead, 2)
        if h == 2 and in_step:
            mixed_grads[0], other = lax.optimization_barrier((mixed_grads[0], other))
            keep, other = scatter(add_low(keep, other), 1)
        earlier = []
        if h:
            earlier = [dps[0], extra]
        if h == heads - 1:
            earlier += dps[1:]
        *dp, payload, extra = head_gradients(h, mixed_grads, earlier)
        dps += dp
        payloads.append(payload)
    normed_near, normed_send = dps[-2:]
    small = jnp.concatenate([norm2_grad, router_grad])
    small = jnp.concatenate([small, extra[:2], jnp.zeros((-(experts + 3) % 16, D), F32)])
    count = small.shape[0]
    wide = jnp.concatenate(payloads[1:])
    normed_other = over_core(normed_send)
    out_grad_far = over_x(after(out_grad_far, branch2))

    def with_small(send, bit):
        got = swap(jnp.concatenate([send, small.astype(BF16)]), "expert", bit)
        return got[:-count], got[-count:].astype(F32)

    if in_step:
        ahead = add_low(keep, other)
        keep, send = halves(wide, 1)
        got, more = with_small(send, 1)
        ahead_other = swap(ahead, "expert", 4)
        got, more, ahead_other, normed_other, out_grad_far = lax.optimization_barrier(
            (got, more, ahead_other, normed_other, out_grad_far)
        )
        wide, small = add_low(keep, got), small + more
        ahead = add_low(ahead, ahead_other)
    near = normed_near + normed_other.astype(F32)
    normed_other = over_x(near[1].astype(BF16))
    expert_in_grad = (dot(rows, upward_own, 0, 0) + in_grad_far.astype(F32))[None]
    if in_step:
        keep, send = halves(wide, 2)
        got, more = with_small(send, 2)
        ahead_other = swap(ahead, "expert", 1)
        got, more, ahead_other, normed_other, expert_in_grad = lax.optimization_barrier(
            (got, more, ahead_other, normed_other, expert_in_grad)
        )
        wide, small = add_low(keep, got), small + more
        ahead = joined(ahead, ahead_other, 1)
    normed_grad = near[0] + normed_other.astype(F32)
    scaled1 = normed_grad * norm1_gain
    input_grad = (
        hidden_grad
        + s1 * scaled1
        - inputs * s1**3 * jnp.mean(scaled1 * inputs, axis=-1, keepdims=True)
    )
    expert_out_grad = (dot(active_own, grads, 0, 0) + out_grad_far.astype(F32))[None]
    if in_step:
        got, more = with_small(wide, 4)
        ahead_other = swap(ahead, "expert", 2)
        got, more, ahead_other, input_grad, expert_out_grad = lax.optimization_barrier(
            (got, more, ahead_other, input_grad, expert_out_grad)
        )
        wide, small = add_low(wide, got), small + more
        ahead = joined(ahead, ahead_other, 2)
    else:
        wide, ahead, small = lax.psum((wide.astype(F32), ahead.astype(F32), small), "expert")
    small_other = over_x(small)
    if in_step:
        got = swap(wide, "expert", 2)
        got, small_other = lax.optimization_barrier((got, small_other))
        wide = joined(wide, got, 2)
    small = small + small_other
    small_other = over_core(small)
    if in_step:
        wide = joined(wide, swap(wide, "expert", 1), 1)
    small = small + small_other
    qkv_grad = jnp.concatenate([ahead[: 3 * HEAD_DIM], wide])
    qkv_grad = jnp.transpose(qkv_grad.reshape(heads, 3, HEAD_DIM, D), (1, 3, 0, 2))
    qkv_grad = qkv_grad.reshape(3, D, width).astype(F32)
    norm1_grad = small[experts + 1]
    table_size = BUCKETS * heads
    table_grad = lax.dynamic_slice_in_dim(small[experts + 2], me[0] * table_size, table_size)
    table_grad = table_grad.reshape(BUCKETS, heads)
    return (
        output,
        input_grad,
        norm1_grad,
        qkv_grad,
        ahead[3 * HEAD_DIM :].astype(F32),
        table_grad,
        small[0],
        jnp.transpose(small[1 : experts + 1]),
        expert_in_grad,
        expert_out_grad,
    )


def solution(mesh):
    placed = (
        P(("expert", "shard"), None),
        P(),
        P(None, None, "shard"),
        P("shard", None),
        P(None, "shard"),
        P(),
        P(),
        P("expert", None, "shard"),
        P("expert", "shard", None),
        P("expert"),
        P(("expert", "shard")),
        P(("expert", "shard")),
        P(("expert", "shard"), None),
    )
    return jax.shard_map(
        shards,
        mesh=mesh,
        in_specs=placed,
        out_specs=(
            P(("expert", "shard"), None),
            P(("expert", "shard"), None),
            P(),
            P(None, None, "shard"),
            P("shard", None),
            P(None, "shard"),
            P(),
            P(),
            P("expert", None, "shard"),
            P("expert", "shard", None),
        ),
        check_vma=False,
    )
```

```python
import functools

import jax
import jax.numpy as jnp
from jax import lax
from jax.experimental import pallas as pl
from jax.experimental.pallas import tpu as pltpu
from jax.sharding import PartitionSpec as P

D = 768
HEAD_DIM = 64
BUCKETS = 32


EPS = 1e-06
THRESHOLDS = (12, 16, 23, 32, 46, 64, 91)
NEG = -1000000000.0
F32 = jnp.float32
ORDER = (6, 7, 4, 2, 3, 1, 5, 0)
BF16 = jnp.bfloat16


def bucket_of(relative):
    distance = jnp.abs(relative)
    far = 8 + sum(((distance >= edge).astype(jnp.int32) for edge in THRESHOLDS))
    near = jnp.where(distance < 8, distance, jnp.minimum(far, 15))
    return near + jnp.where(relative > 0, 16, 0)


def rms_norm(values, gain):
    return values * lax.rsqrt(jnp.mean(values * values, axis=-1, keepdims=True) + EPS) * gain


def gelu_tanh(values):
    return jax.nn.gelu(values, approximate=True)


def dot(a, b, ca=1, cb=0):
    return lax.dot_general(a, b, (((ca,), (cb,)), ((), ())), preferred_element_type=F32)


def swap(x, axis, bit):
    size = lax.axis_size(axis)
    return lax.ppermute(x, axis, [(i, i ^ bit) for i in range(size)])


def after(x, *others):
    return lax.optimization_barrier((x, *others))[0]


def exchange(rows):
    size = lax.axis_size("expert")
    count = rows.shape[0] // size
    if size != 8:
        return lax.all_to_all(rows, "expert", split_axis=0, concat_axis=0, tiled=True)
    blocks = [rows[k * count : (k + 1) * count] for k in range(size)]
    blocks = [swap(x, "expert", k) if k else x for k, x in zip(ORDER, blocks)]
    return jnp.concatenate(blocks)


def build_bias(table_ref, head, tiles_ref, tok):
    wide = 4 * tok
    row = lax.broadcasted_iota(jnp.int32, (8, wide), 0)
    col = lax.broadcasted_iota(jnp.int32, (8, wide), 1)
    relative = col - tok - row - jnp.where(col >= 3 * tok, wide, 0)
    bucket = bucket_of(relative)
    base = jnp.zeros((8, wide), F32)
    for b in range(BUCKETS):
        base = jnp.where(bucket == b, table_ref[b, head], base)
    for a in range(tok // 8):
        rows = pltpu.roll(base, 8 * a, 1) if a else base
        for d in range(3):
            tiles_ref[d + 1, 8 * a : 8 * a + 8, :] = rows[:, d * tok : (d + 1) * tok]
    tiles_ref[0] = jnp.full((tok, tok), table_ref[15, head], F32)
    tiles_ref[4] = jnp.full((tok, tok), table_ref[31, head], F32)


def tile_index(me, j, l):
    return jnp.clip((me ^ l) - (me ^ j), -2, 2) + 2


def masked_scores(me, j, q, keys, tiles_ref, seg_col, seg_row_ref, blocks, tok):
    parts = []
    for l in range(blocks):
        s = dot(q, keys[:, l * tok : (l + 1) * tok])
        s = s + tiles_ref[tile_index(me, j, l)]
        parts.append(jnp.where(seg_col == seg_row_ref[me ^ l], s, NEG))
    return parts


def forward_kernel(
    me_ref, table_ref, seg_row_ref, seg_col_ref, x0, x1, x2a, x2b, x3a, x3b, w_ref,
    proj_ref, lse_ref, m0, m1, m2, m3, tiles_ref, mixed_ref, kt_ref,
):
    me = me_ref[0]
    heads = table_ref.shape[1]
    tok = x0.shape[0]
    half = tok // 2
    pieces = ((x0, 0), (x1, tok), (x2a, 2 * tok), (x2b, 2 * tok + half), (x3a, 3 * tok), (x3b, 3 * tok + half))
    for ref, start in pieces:
        rows = ref.shape[0]
        projected = dot(ref[...], w_ref[...], 1, 1).astype(BF16)
        for which in range(3):
            for h in range(heads):
                at = (3 * h + which) * HEAD_DIM
                part = projected[:, at : at + HEAD_DIM]
                if which == 0:
                    part = part * jnp.asarray(0.125, BF16)
                proj_ref[which, h, start : start + rows, :] = part
    for h in range(heads):
        build_bias(table_ref, h, tiles_ref, tok)

        kt_ref[...] = proj_ref[1, h].astype(F32).T.astype(BF16)

        def block(j, carry):
            q = proj_ref[0, h, pl.ds(pl.multiple_of(j * tok, tok), tok), :]
            keys = kt_ref[...]
            seg_col = seg_col_ref[me ^ j]
            parts = masked_scores(me, j, q, keys, tiles_ref, seg_col, seg_row_ref, 4, tok)
            top = functools.reduce(jnp.maximum, parts)
            top = jnp.max(top, axis=1, keepdims=True)
            probs = [jnp.exp(s - top) for s in parts]
            total = jnp.sum(functools.reduce(jnp.add, probs), axis=1, keepdims=True)
            mixed = None
            for l in range(4):
                term = dot(probs[l].astype(BF16), proj_ref[2, h, l * tok : (l + 1) * tok, :])
                mixed = term if mixed is None else mixed + term
            mixed_ref[h, pl.ds(pl.multiple_of(j * tok, tok), tok), :] = (mixed / total).astype(BF16)
            lse_ref[h, pl.ds(pl.multiple_of(j * tok, tok), tok), :] = jnp.broadcast_to(
                top + jnp.log(total), (tok, 128)
            )
            return carry

        lax.fori_loop(0, 4, block, 0, unroll=4)
    for j, out in enumerate((m0, m1, m2, m3)):
        out[...] = jnp.concatenate(
            [mixed_ref[h, j * tok : (j + 1) * tok, :] for h in range(heads)], axis=1
        )


def backward_kernel(
    h, final, me_ref, table_ref, seg_row_ref, seg_col_ref, x0, x1, x2a, x2b, x3a, x3b, w_ref, gain_ref,
    proj_ref, lse_ref, g0, g1, g2, g3, *rest,
):
    me = me_ref[0]
    heads = table_ref.shape[1]
    tok = x0.shape[0]
    half = tok // 2
    if h:
        earlier, extra_before, *rest = rest
    dp_before, rest = (rest[: h - 1], rest[h - 1 :]) if final else ((), rest)
    if final:
        normed_near_ref, normed_send_ref, *rest = rest
    else:
        dp_out, *rest = rest
    payload_ref, extra_ref, tiles_ref, sums_ref, do_ref, dkt_ref, dvt_ref, dp_ref, dpt_ref, kt_ref, vt_ref = rest
    width = HEAD_DIM
    for j, ref in enumerate((g0, g1, g2, g3)):
        do_ref[j * tok : (j + 1) * tok, :] = ref[:, h * width : (h + 1) * width]
    build_bias(table_ref, h, tiles_ref, tok)
    sums_ref[...] = jnp.zeros_like(sums_ref)
    dkt_ref[...] = jnp.zeros_like(dkt_ref)
    dvt_ref[...] = jnp.zeros_like(dvt_ref)

    kt_ref[...] = proj_ref[1, 0].astype(F32).T.astype(BF16)
    vt_ref[...] = proj_ref[2, 0].astype(F32).T.astype(BF16)

    def block(j, carry):
        rows = pl.ds(pl.multiple_of(j * tok, tok), tok)
        q = proj_ref[0, 0, rows, :]
        grad = do_ref[rows, :]
        q_t = q.astype(F32).T.astype(BF16)
        grad_t = grad.astype(F32).T.astype(BF16)
        seg_col = seg_col_ref[me ^ j]
        parts = masked_scores(me, j, q, kt_ref[...], tiles_ref, seg_col, seg_row_ref, 4, tok)
        lse = lse_ref[0, rows, :][:, :1]
        probs, weighted = [], []
        for l in range(4):
            p = jnp.exp(parts[l] - lse)
            cut = slice(l * tok, (l + 1) * tok)
            dvt_ref[:, cut] += dot(grad_t, p.astype(BF16))
            probs.append(p)
            weighted.append(p * dot(grad, vt_ref[:, cut]))
        delta = jnp.sum(functools.reduce(jnp.add, weighted), axis=1, keepdims=True)
        dq = None
        for l in range(4):
            cut = slice(l * tok, (l + 1) * tok)
            ds = weighted[l] - probs[l] * delta
            at = tile_index(me, j, l)
            sums_ref[at] = sums_ref[at] + ds
            low = ds.astype(BF16)
            dkt_ref[:, cut] += dot(q_t, low)
            term = dot(low, proj_ref[1, 0, cut, :])
            dq = term if dq is None else dq + term
        dq = dq * 0.125
        dp_ref[rows, :width] = dq.astype(BF16)
        dpt_ref[j, :width, :] = dq.T.astype(BF16)
        return carry

    lax.fori_loop(0, 4, block, 0, unroll=4)
    dkt = dkt_ref[...]
    dvt = dvt_ref[...]
    dp_ref[:, width : 2 * width] = dkt.T.astype(BF16)
    dp_ref[:, 2 * width :] = dvt.T.astype(BF16)
    for j in range(4):
        cut = slice(j * tok, (j + 1) * tok)
        dpt_ref[j, width : 2 * width, :] = dkt[:, cut].astype(BF16)
        dpt_ref[j, 2 * width :, :] = dvt[:, cut].astype(BF16)

    strip = jnp.concatenate([sums_ref[1], sums_ref[2], sums_ref[3], jnp.zeros((tok, tok), F32)], axis=1)
    rows = tok
    while rows > 8:
        rows //= 2
        strip = strip[:rows] + pltpu.roll(strip[rows:], 4 * tok - rows, 1)
    diagonal = strip[0:1]
    for i in range(1, 8):
        diagonal = diagonal + pltpu.roll(strip[i : i + 1], 4 * tok - i, 1)
    col = lax.broadcasted_iota(jnp.int32, (1, 4 * tok), 1)
    bucket = bucket_of(col - tok - jnp.where(col >= 3 * tok, 4 * tok, 0))
    low_far = jnp.sum(jnp.sum(sums_ref[0], axis=0, keepdims=True), axis=1, keepdims=True)
    high_far = jnp.sum(jnp.sum(sums_ref[4], axis=0, keepdims=True), axis=1, keepdims=True)
    entry = lax.broadcasted_iota(jnp.int32, (BUCKETS, 1), 0)
    values = jnp.sum(jnp.where(bucket == entry, diagonal, 0.0), axis=1, keepdims=True)
    values = values + jnp.where(entry == 15, low_far, 0.0) + jnp.where(entry == 31, high_far, 0.0)
    lane = lax.broadcasted_iota(jnp.int32, (BUCKETS, D), 1) - me * (BUCKETS * heads)
    at = lax.broadcasted_iota(jnp.int32, (BUCKETS, D), 0) * heads + h
    table_row = jnp.sum(jnp.where(lane == at, values, 0.0), axis=0, keepdims=True)

    pieces = ((x0, 0, 0), (x1, 1, 0), (x2a, 2, 0), (x2b, 2, half), (x3a, 3, 0), (x3b, 3, half))
    total = None
    for ref, j, start in pieces:
        term = dot(dpt_ref[j, :, start : start + ref.shape[0]], ref[...])
        total = term if total is None else total + term
    payload_ref[...] = total.astype(BF16)
    gain_row = jnp.sum(total * w_ref[h].astype(F32), axis=0, keepdims=True) / gain_ref[...]
    row = lax.broadcasted_iota(jnp.int32, (8, D), 0)
    extra = jnp.where(row == 0, gain_row, jnp.where(row == 1, table_row, 0.0))
    extra_ref[...] = extra + extra_before[...] if h else extra
    if final:
        for j in range(4):
            cut = slice(j * tok, (j + 1) * tok)
            part = dot(dp_ref[cut, :], w_ref[h])
            for i, ref in enumerate((earlier, *dp_before)[: h]):
                part = part + dot(ref[cut, :], w_ref[i])
            if j % 2:
                normed_send_ref[j // 2] = part.astype(BF16)
            else:
                normed_near_ref[j // 2] = part
    else:
        dp_out[...] = dp_ref[...]


def hidden_units(rows_ref, grads_ref, w_in, w_out, active_ref, upward_ref):
    wide = 256
    count = rows_ref.shape[0] // 2
    c0, c1 = 0.7978845608028654, 0.044715
    for at in range(0, w_in.shape[1], wide):
        cut = slice(at, at + wide)
        for r in range(0, 2 * count, count):
            part = slice(r, r + count)
            v = dot(rows_ref[part, :], w_in[:, cut])
            square = v * v
            t = jnp.tanh(c0 * (v + c1 * (square * v)))
            half = 0.5 + 0.5 * t
            active_ref[part, cut] = (v * half).astype(BF16)
            slope = half + (0.5 * c0) * v * (1.0 - t * t) * (1.0 + (3.0 * c1) * square)
            grad = dot(grads_ref[part, :], w_out[cut, :], 1, 1)
            upward_ref[part, cut] = (grad * slope).astype(BF16)


def expert_own_kernel(
    near_ref, beside_ref, in_own, out_own, active_own, upward_own, rows_ref, grads_ref, sums_ref
):
    count = near_ref.shape[0]
    rows_ref[:count, :] = near_ref[:, :D]
    rows_ref[count:, :] = beside_ref[:, :D]
    grads_ref[:count, :] = near_ref[:, D:]
    grads_ref[count:, :] = beside_ref[:, D:]
    hidden_units(rows_ref, grads_ref, in_own, out_own, active_own, upward_own)
    wide = 256
    for at in range(0, D, wide):
        cut = slice(at, at + wide)
        into = slice(D + at, D + at + wide)
        for r in (0, count):
            part = slice(r, r + count)
            sums_ref[part, cut] = dot(active_own[part, :], out_own[:, cut])
            sums_ref[part, into] = dot(upward_own[part, :], in_own[cut, :], 1, 1)


def expert_far_kernel(
    far_a, far_b, far_c, out_a, out_b, rows_ref, grads_ref, sums_ref,
    in_grad_far, out_grad_far, mine_ref, theirs_ref, active_far, upward_far, in_far, out_far,
):
    count = mine_ref.shape[0]
    for whole, pieces in ((in_far, (far_a, far_b, far_c)), (out_far, (out_a, out_b))):
        at = 0
        for ref in pieces:
            whole[at : at + ref.shape[0], :] = ref[...]
            at += ref.shape[0]
    hidden_units(rows_ref, grads_ref, in_far, out_far, active_far, upward_far)
    wide = 256
    for at in range(0, D, wide):
        cut = slice(at, at + wide)
        into = slice(D + at, D + at + wide)
        for r in (count, 0):
            part = slice(r, r + count)
            produced = sums_ref[part, cut] + dot(active_far[part, :], out_far[:, cut])
            row_grad = sums_ref[part, into] + dot(upward_far[part, :], in_far[cut, :], 1, 1)
            if r:
                theirs_ref[:, cut] = produced.astype(BF16)
                theirs_ref[:, into] = row_grad.astype(BF16)
            else:
                mine_ref[:, cut] = produced
                mine_ref[:, into] = row_grad
        in_grad_far[:, cut] = dot(rows_ref[...], upward_far[:, cut], 0, 0).astype(BF16)
        out_grad_far[:, cut] = dot(active_far[...], grads_ref[:, cut], 0, 0).astype(BF16)


VMEM = pl.BlockSpec(memory_space=pltpu.VMEM)
SMEM = pl.BlockSpec(memory_space=pltpu.SMEM)
PARAMS = pltpu.CompilerParams(vmem_limit_bytes=24 * 1024 * 1024)


def halves(x, bit):
    n = x.shape[0] // 2
    upper = (lax.axis_index("expert") & bit) != 0
    keep = jnp.where(upper, x[n:], x[:n])
    send = jnp.where(upper, x[:n], x[n:])
    return keep, send


def add_low(a, b):
    return (a.astype(F32) + b.astype(F32)).astype(BF16)


def joined(x, other, bit):
    upper = (lax.axis_index("expert") & bit) != 0
    return jnp.concatenate([jnp.where(upper, other, x), jnp.where(upper, x, other)])


def shards(
    tokens,
    norm1_gain,
    qkv_weight,
    out_weight,
    bucket_position_bias,
    norm2_gain,
    router_weight,
    expert_in,
    expert_out,
    segment,
    route,
    slot,
    cotangent,
):
    highest_precision = lax.Precision.HIGHEST
    tok = tokens.shape[0]
    half = tok // 2
    seq = segment.shape[0]
    experts = router_weight.shape[1]
    capacity = (5 * tok + 4 * experts - 1) // (4 * experts)
    heads = bucket_position_bias.shape[1]
    width = out_weight.shape[0]
    me = lax.axis_index("shard").astype(jnp.int32).reshape(1)
    sources = lax.axis_size("expert")

    def over_x(v):
        return swap(v, "shard", 2)

    def over_core(v):
        return swap(v, "shard", 1)

    inputs = tokens.astype(F32)
    s1 = lax.rsqrt(jnp.mean(inputs * inputs, axis=-1, keepdims=True) + EPS)
    normed_low = (inputs * s1 * norm1_gain).astype(BF16)
    x2a = over_x(normed_low[:half])
    x2b = over_x(normed_low[half:])
    x1 = over_core(normed_low)
    x3a = over_core(x2a)
    x3b = over_core(x2b)
    pieces = (normed_low, x1, x2a, x2b, x3a, x3b)
    out_w1 = over_core(out_weight)
    out_w2 = over_x(out_weight)
    in_own, out_own = expert_in[0], expert_out[0]
    split = 13 * D // 24
    split_again = 3 * D // 4
    in_far = over_x(after(in_own[:split], x2b))
    qkv_t = jnp.transpose(qkv_weight.reshape(3, D, heads, HEAD_DIM), (2, 0, 3, 1))
    qkv_t = qkv_t.reshape(heads, 3 * HEAD_DIM, D)
    seg_rows = segment.reshape(4, 1, tok)
    seg_cols = segment.reshape(4, tok, 1)

    sds = jax.ShapeDtypeStruct
    proj, lse, *mixed = pl.pallas_call(
        forward_kernel,
        out_shape=[sds((3, heads, seq, HEAD_DIM), BF16), sds((heads, seq, 128), F32)]
        + [sds((tok, width), BF16)] * 4,
        in_specs=[SMEM, SMEM] + [VMEM] * 9,
        out_specs=[VMEM] * 6,
        scratch_shapes=[
            pltpu.VMEM((5, tok, tok), F32),
            pltpu.VMEM((heads, seq, HEAD_DIM), BF16),
            pltpu.VMEM((HEAD_DIM, seq), BF16),
        ],
        compiler_params=PARAMS,
        cost_estimate=pl.CostEstimate(flops=15 * 10**9, bytes_accessed=8 * 10**6, transcendentals=3 * 10**6),
        name="attention_forward",
    )(me, bucket_position_bias, seg_rows, seg_cols, *pieces, qkv_t.reshape(3 * width, D))

    *mixed, out_w2, in_far = lax.optimization_barrier((*mixed, out_w2, in_far))
    out_w3 = over_core(out_w2)
    out_w = jnp.concatenate([out_weight, out_w1, out_w2, out_w3])
    mixed_in = [swap(mixed[k], "shard", k) for k in (1, 2, 3)]
    in_rest = over_x(after(in_own[split:split_again], mixed_in[0]))
    in_last = over_x(after(in_own[split_again:], mixed_in[0]))
    split_out = 2 * D // 3
    out_far = over_x(after(out_own[:split_out], mixed_in[0]))
    mixed_own = jnp.concatenate([mixed[0]] + mixed_in, axis=1)
    attended = dot(mixed_own, out_w)
    hidden = inputs + attended
    s2 = lax.rsqrt(jnp.mean(hidden * hidden, axis=-1, keepdims=True) + EPS)
    routed_low = (hidden * s2 * norm2_gain).astype(BF16)
    routed_full = routed_low.astype(F32)
    chosen = (route[:, None] == jnp.arange(experts, dtype=jnp.int32)[None, :]).astype(F32)
    router_probs = jax.nn.softmax(jnp.dot(routed_full, router_weight, precision=highest_precision), axis=-1)
    gate = jnp.sum(router_probs * chosen, axis=-1, keepdims=True)
    upstream = cotangent.astype(F32)

    columns = jnp.arange(experts * capacity, dtype=jnp.int32)
    if sources == 8 == experts:
        order = jnp.repeat(jnp.asarray(ORDER, jnp.int32), capacity) ^ lax.axis_index("expert")
        columns = order * capacity + columns % capacity
    placed = ((route * capacity + slot)[:, None] == columns[None, :]) & (slot[:, None] >= 0)
    dispatch = placed.astype(BF16)
    both = jnp.concatenate([routed_low, (gate * upstream).astype(BF16)], axis=1)
    outgoing = dot(dispatch, both, 0, 0).astype(BF16)
    outgoing, in_rest = lax.optimization_barrier((outgoing, in_rest))
    arrived = exchange(outgoing)
    in_last, out_far, arrived = lax.optimization_barrier((in_last, out_far, arrived))
    out_last = over_x(after(out_own[split_out:], out_far))
    beside = over_core(arrived)
    count = experts * capacity

    active_own, upward_own, rows, grads, sums = pl.pallas_call(
        expert_own_kernel,
        out_shape=[sds((2 * count, D), BF16)] * 4 + [sds((2 * count, 2 * D), F32)],
        in_specs=[VMEM] * 4,
        out_specs=[VMEM] * 5,
        compiler_params=PARAMS,
        cost_estimate=pl.CostEstimate(flops=3 * 10**9, bytes_accessed=6 * 10**6, transcendentals=5 * 10**5),
        name="expert_own",
    )(arrived, beside, in_own, out_own)
    in_grad_far, out_grad_far, mine, theirs = pl.pallas_call(
        expert_far_kernel,
        out_shape=[sds((D, D), BF16)] * 2 + [sds((count, 2 * D), F32), sds((count, 2 * D), BF16)],
        in_specs=[VMEM] * 8,
        out_specs=[VMEM] * 4,
        scratch_shapes=[pltpu.VMEM((2 * count, D), BF16)] * 2 + [pltpu.VMEM((D, D), BF16)] * 2,
        compiler_params=PARAMS,
        cost_estimate=pl.CostEstimate(flops=5 * 10**9, bytes_accessed=6 * 10**6, transcendentals=5 * 10**5),
        name="expert_far",
    )(in_far, in_rest, in_last, out_far, out_last, rows, grads, sums)
    in_grad_far = over_x(in_grad_far)
    returned = exchange(add_low(mine, over_core(theirs)))
    returned, in_grad_far = lax.optimization_barrier((returned, in_grad_far))
    back = dot(dispatch, returned)
    combined, expert_grad = back[:, :D], back[:, D:]
    output = (hidden + gate * combined).astype(BF16)
    gate_grad = jnp.sum(upstream * combined, axis=-1, keepdims=True)
    logit_grad = router_probs * (gate_grad * chosen - gate_grad * gate)
    router_grad = lax.dot_general(
        logit_grad, routed_full, (((0,), (0,)), ((), ())), precision=highest_precision
    )
    routed_grad = expert_grad + lax.dot_general(
        logit_grad, router_weight, (((1,), (1,)), ((), ())), precision=highest_precision
    )
    norm2_grad = jnp.sum(routed_grad * hidden * s2, axis=0, keepdims=True)
    scaled = routed_grad * norm2_gain
    hidden_grad = (
        upstream + s2 * scaled - hidden * s2**3 * jnp.mean(scaled * hidden, axis=-1, keepdims=True)
    )
    branch_low = hidden_grad.astype(BF16)
    mixed_grad = dot(branch_low, out_w, 1, 1).astype(BF16)
    mixed_grads = [mixed_grad[:, :width]] + [
        swap(mixed_grad[:, k * width : (k + 1) * width], "shard", k) for k in (1, 2, 3)
    ]
    branch1 = over_core(branch_low)
    branch2 = over_x(after(branch_low, mixed_grads[1]))
    third = D // 3
    out_grad_a = over_x(after(out_grad_far[:third], mixed_grads[1]))
    def head_gradients(h, grads, earlier):
        final = h == heads - 1
        one = pl.BlockSpec((3, 1, seq, HEAD_DIM), lambda i: (0, h, 0, 0))
        log = pl.BlockSpec((1, seq, 128), lambda i: (h, 0, 0))
        return pl.pallas_call(
            functools.partial(backward_kernel, h, final),
            grid=(1,),
            out_shape=[sds((2, tok, D), F32), sds((2, tok, D), BF16)] * final
            + [sds((seq, 3 * HEAD_DIM), BF16)] * (not final)
            + [
                sds((3 * HEAD_DIM, D), BF16),
                sds((8, D), F32),
            ],
            in_specs=[SMEM, SMEM] + [VMEM] * 10 + [one, log] + [VMEM] * (4 + len(earlier)),
            out_specs=[VMEM] * (3 + final),
            scratch_shapes=[
                pltpu.VMEM((5, tok, tok), F32),
                pltpu.VMEM((5, tok, tok), F32),
                pltpu.VMEM((seq, HEAD_DIM), BF16),
                pltpu.VMEM((HEAD_DIM, seq), F32),
                pltpu.VMEM((HEAD_DIM, seq), F32),
                pltpu.VMEM((seq, 3 * HEAD_DIM), BF16),
                pltpu.VMEM((4, 3 * HEAD_DIM, tok), BF16),
                pltpu.VMEM((HEAD_DIM, seq), BF16),
                pltpu.VMEM((HEAD_DIM, seq), BF16),
            ],
            compiler_params=PARAMS,
            cost_estimate=pl.CostEstimate(flops=8 * 10**9, bytes_accessed=6 * 10**6, transcendentals=10**6),
            name="attention_backward_%d" % h,
        )(
            me, bucket_position_bias, seg_rows, seg_cols, *pieces, qkv_t, norm1_gain.reshape(1, D),
            proj, lse, *grads, *earlier,
        )

    in_step = sources == 8

    def scatter(part, bit):
        keep, send = halves(part, bit)
        return keep, swap(send, "expert", bit)

    dps, payloads, extra = [], [], None
    for h in range(heads):
        if h == heads - 1:
            mixed_grads[0], branch2, out_grad_a = lax.optimization_barrier(
                (mixed_grads[0], branch2, out_grad_a)
            )
            out_grad_b = over_x(after(out_grad_far[third:], out_grad_a))
            branch3 = over_core(branch2)
            branches = (branch_low, branch1, branch2, branch3)
            out_grad = sum(dot(mixed[k], b, 0, 0) for k, b in enumerate(branches))
            ahead = jnp.concatenate([payloads[0], out_grad.astype(BF16)])
            if in_step:
                keep, send = halves(ahead, 2)
                mixed_grads[0], keep, send = lax.optimization_barrier((mixed_grads[0], keep, send))
                other = swap(send, "expert", 2)
        earlier = []
        if h:
            earlier = [dps[0], extra]
        if h == heads - 1:
            earlier += dps[1:]
        *dp, payload, extra = head_gradients(h, mixed_grads, earlier)
        dps += dp
        payloads.append(payload)
    normed_near, normed_send = dps[-2:]
    small = jnp.concatenate([norm2_grad, router_grad])
    small = jnp.concatenate([small, extra[:2], jnp.zeros((-(experts + 3) % 16, D), F32)])
    count = small.shape[0]
    wide = jnp.concatenate(payloads[1:])
    normed_other = over_core(normed_send)

    def with_small(send, bit):
        got = swap(jnp.concatenate([send, small.astype(BF16)]), "expert", bit)
        return got[:-count], got[-count:].astype(F32)

    if in_step:
        ahead_keep, ahead_other = scatter(add_low(keep, other), 1)
        keep, send = halves(wide, 2)
        got, more = with_small(send, 2)
        got, more, ahead_other, normed_other, out_grad_b, in_grad_far = lax.optimization_barrier(
            (got, more, ahead_other, normed_other, out_grad_b, in_grad_far)
        )
        wide, small = add_low(keep, got), small + more
        ahead = add_low(ahead_keep, ahead_other)
    near = normed_near + normed_other.astype(F32)
    normed_other = over_x(near[1].astype(BF16))
    expert_in_grad = (dot(rows, upward_own, 0, 0) + in_grad_far.astype(F32))[None]
    if in_step:
        keep, send = halves(wide, 1)
        got, more = with_small(send, 1)
        ahead_other = swap(ahead, "expert", 4)
        got, more, ahead_other, normed_other, out_grad_a, expert_in_grad = lax.optimization_barrier(
            (got, more, ahead_other, normed_other, out_grad_a, expert_in_grad)
        )
        wide, small = add_low(keep, got), small + more
        ahead = add_low(ahead, ahead_other)
    normed_grad = near[0] + normed_other.astype(F32)
    scaled1 = normed_grad * norm1_gain
    input_grad = (
        hidden_grad
        + s1 * scaled1
        - inputs * s1**3 * jnp.mean(scaled1 * inputs, axis=-1, keepdims=True)
    )
    out_grad_far = jnp.concatenate([out_grad_a, out_grad_b])
    expert_out_grad = (dot(active_own, grads, 0, 0) + out_grad_far.astype(F32))[None]
    if in_step:
        got, more = with_small(wide, 4)
        ahead_other = swap(ahead, "expert", 1)
        got, more, ahead_other, input_grad, expert_out_grad = lax.optimization_barrier(
            (got, more, ahead_other, input_grad, expert_out_grad)
        )
        wide, small = add_low(wide, got), small + more
        ahead = joined(ahead, ahead_other, 1)
    else:
        wide, ahead, small = lax.psum((wide.astype(F32), ahead.astype(F32), small), "expert")
    small_other = over_x(small)
    if in_step:
        got, ahead_other = swap(wide, "expert", 1), swap(ahead, "expert", 2)
        got, ahead_other, small_other = lax.optimization_barrier((got, ahead_other, small_other))
        wide = joined(wide, got, 1)
        ahead = joined(ahead, ahead_other, 2)
    small = small + small_other
    small_other = over_core(small)
    if in_step:
        wide = joined(wide, swap(wide, "expert", 2), 2)
    small = small + small_other
    qkv_grad = jnp.concatenate([ahead[: 3 * HEAD_DIM], wide])
    qkv_grad = jnp.transpose(qkv_grad.reshape(heads, 3, HEAD_DIM, D), (1, 3, 0, 2))
    qkv_grad = qkv_grad.reshape(3, D, width).astype(F32)
    norm1_grad = small[experts + 1]
    table_size = BUCKETS * heads
    table_grad = lax.dynamic_slice_in_dim(small[experts + 2], me[0] * table_size, table_size)
    table_grad = table_grad.reshape(BUCKETS, heads)
    return (
        output,
        input_grad,
        norm1_grad,
        qkv_grad,
        ahead[3 * HEAD_DIM :].astype(F32),
        table_grad,
        small[0],
        jnp.transpose(small[1 : experts + 1]),
        expert_in_grad,
        expert_out_grad,
    )


def solution(mesh):
    placed = (
        P(("expert", "shard"), None),
        P(),
        P(None, None, "shard"),
        P("shard", None),
        P(None, "shard"),
        P(),
        P(),
        P("expert", None, "shard"),
        P("expert", "shard", None),
        P("expert"),
        P(("expert", "shard")),
        P(("expert", "shard")),
        P(("expert", "shard"), None),
    )
    return jax.shard_map(
        shards,
        mesh=mesh,
        in_specs=placed,
        out_specs=(
            P(("expert", "shard"), None),
            P(("expert", "shard"), None),
            P(),
            P(None, None, "shard"),
            P("shard", None),
            P(None, "shard"),
            P(),
            P(),
            P("expert", None, "shard"),
            P("expert", "shard", None),
        ),
        check_vma=False,
    )
```

```python
import functools

import jax
import jax.numpy as jnp
from jax import lax
from jax.experimental import pallas as pl
from jax.experimental.pallas import tpu as pltpu
from jax.sharding import PartitionSpec as P

D = 768
HEAD_DIM = 64
BUCKETS = 32


EPS = 1e-06
THRESHOLDS = (12, 16, 23, 32, 46, 64, 91)
NEG = -1000000000.0
F32 = jnp.float32
ORDER = (6, 7, 4, 2, 3, 1, 5, 0)
BF16 = jnp.bfloat16


def bucket_of(relative):
    distance = jnp.abs(relative)
    far = 8 + sum(((distance >= edge).astype(jnp.int32) for edge in THRESHOLDS))
    near = jnp.where(distance < 8, distance, jnp.minimum(far, 15))
    return near + jnp.where(relative > 0, 16, 0)


def rms_norm(values, gain):
    return values * lax.rsqrt(jnp.mean(values * values, axis=-1, keepdims=True) + EPS) * gain


def gelu_tanh(values):
    return jax.nn.gelu(values, approximate=True)


def dot(a, b, ca=1, cb=0):
    return lax.dot_general(a, b, (((ca,), (cb,)), ((), ())), preferred_element_type=F32)


def swap(x, axis, bit):
    size = lax.axis_size(axis)
    return lax.ppermute(x, axis, [(i, i ^ bit) for i in range(size)])


def after(x, *others):
    return lax.optimization_barrier((x, *others))[0]


def exchange(rows):
    size = lax.axis_size("expert")
    count = rows.shape[0] // size
    if size != 8:
        return lax.all_to_all(rows, "expert", split_axis=0, concat_axis=0, tiled=True)
    blocks = [rows[k * count : (k + 1) * count] for k in range(size)]
    blocks = [swap(x, "expert", k) if k else x for k, x in zip(ORDER, blocks)]
    return jnp.concatenate(blocks)


def build_bias(table_ref, head, tiles_ref, tok):
    wide = 4 * tok
    row = lax.broadcasted_iota(jnp.int32, (8, wide), 0)
    col = lax.broadcasted_iota(jnp.int32, (8, wide), 1)
    relative = col - tok - row - jnp.where(col >= 3 * tok, wide, 0)
    bucket = bucket_of(relative)
    base = jnp.zeros((8, wide), F32)
    for b in range(BUCKETS):
        base = jnp.where(bucket == b, table_ref[b, head], base)
    for a in range(tok // 8):
        rows = pltpu.roll(base, 8 * a, 1) if a else base
        for d in range(3):
            tiles_ref[d + 1, 8 * a : 8 * a + 8, :] = rows[:, d * tok : (d + 1) * tok]
    tiles_ref[0] = jnp.full((tok, tok), table_ref[15, head], F32)
    tiles_ref[4] = jnp.full((tok, tok), table_ref[31, head], F32)


def tile_index(me, j, l):
    return jnp.clip((me ^ l) - (me ^ j), -2, 2) + 2


def masked_scores(me, j, q, keys, tiles_ref, seg_col, seg_row_ref, blocks, tok):
    parts = []
    for l in range(blocks):
        s = dot(q, keys[:, l * tok : (l + 1) * tok])
        s = s + tiles_ref[tile_index(me, j, l)]
        parts.append(jnp.where(seg_col == seg_row_ref[me ^ l], s, NEG))
    return parts


def forward_kernel(
    me_ref, table_ref, seg_row_ref, seg_col_ref, x0, x1, x2a, x2b, x3a, x3b, w_ref,
    proj_ref, lse_ref, m0, m1, m2, m3, tiles_ref, mixed_ref, kt_ref,
):
    me = me_ref[0]
    heads = table_ref.shape[1]
    tok = x0.shape[0]
    half = tok // 2
    pieces = ((x0, 0), (x1, tok), (x2a, 2 * tok), (x2b, 2 * tok + half), (x3a, 3 * tok), (x3b, 3 * tok + half))
    for ref, start in pieces:
        rows = ref.shape[0]
        projected = dot(ref[...], w_ref[...], 1, 1).astype(BF16)
        for which in range(3):
            for h in range(heads):
                at = (3 * h + which) * HEAD_DIM
                part = projected[:, at : at + HEAD_DIM]
                if which == 0:
                    part = part * jnp.asarray(0.125, BF16)
                proj_ref[which, h, start : start + rows, :] = part
    for h in range(heads):
        build_bias(table_ref, h, tiles_ref, tok)

        kt_ref[...] = proj_ref[1, h].astype(F32).T.astype(BF16)

        def block(j, carry):
            q = proj_ref[0, h, pl.ds(pl.multiple_of(j * tok, tok), tok), :]
            keys = kt_ref[...]
            seg_col = seg_col_ref[me ^ j]
            parts = masked_scores(me, j, q, keys, tiles_ref, seg_col, seg_row_ref, 4, tok)
            top = functools.reduce(jnp.maximum, parts)
            top = jnp.max(top, axis=1, keepdims=True)
            probs = [jnp.exp(s - top) for s in parts]
            total = jnp.sum(functools.reduce(jnp.add, probs), axis=1, keepdims=True)
            mixed = None
            for l in range(4):
                term = dot(probs[l].astype(BF16), proj_ref[2, h, l * tok : (l + 1) * tok, :])
                mixed = term if mixed is None else mixed + term
            mixed_ref[h, pl.ds(pl.multiple_of(j * tok, tok), tok), :] = (mixed / total).astype(BF16)
            lse_ref[h, pl.ds(pl.multiple_of(j * tok, tok), tok), :] = jnp.broadcast_to(
                top + jnp.log(total), (tok, 128)
            )
            return carry

        lax.fori_loop(0, 4, block, 0, unroll=4)
    for j, out in enumerate((m0, m1, m2, m3)):
        out[...] = jnp.concatenate(
            [mixed_ref[h, j * tok : (j + 1) * tok, :] for h in range(heads)], axis=1
        )


def backward_kernel(
    h, final, me_ref, table_ref, seg_row_ref, seg_col_ref, x0, x1, x2a, x2b, x3a, x3b, w_ref, gain_ref,
    proj_ref, lse_ref, g0, g1, g2, g3, *rest,
):
    me = me_ref[0]
    heads = table_ref.shape[1]
    tok = x0.shape[0]
    half = tok // 2
    if h:
        earlier, extra_before, *rest = rest
    dp_before, rest = (rest[: h - 1], rest[h - 1 :]) if final else ((), rest)
    if final:
        normed_near_ref, normed_send_ref, *rest = rest
    else:
        dp_out, *rest = rest
    payload_ref, extra_ref, tiles_ref, sums_ref, do_ref, dkt_ref, dvt_ref, dp_ref, dpt_ref, kt_ref, vt_ref = rest
    width = HEAD_DIM
    for j, ref in enumerate((g0, g1, g2, g3)):
        do_ref[j * tok : (j + 1) * tok, :] = ref[:, h * width : (h + 1) * width]
    build_bias(table_ref, h, tiles_ref, tok)
    sums_ref[...] = jnp.zeros_like(sums_ref)
    dkt_ref[...] = jnp.zeros_like(dkt_ref)
    dvt_ref[...] = jnp.zeros_like(dvt_ref)

    kt_ref[...] = proj_ref[1, 0].astype(F32).T.astype(BF16)
    vt_ref[...] = proj_ref[2, 0].astype(F32).T.astype(BF16)

    def block(j, carry):
        rows = pl.ds(pl.multiple_of(j * tok, tok), tok)
        q = proj_ref[0, 0, rows, :]
        grad = do_ref[rows, :]
        q_t = q.astype(F32).T.astype(BF16)
        grad_t = grad.astype(F32).T.astype(BF16)
        seg_col = seg_col_ref[me ^ j]
        parts = masked_scores(me, j, q, kt_ref[...], tiles_ref, seg_col, seg_row_ref, 4, tok)
        lse = lse_ref[0, rows, :][:, :1]
        probs, weighted = [], []
        for l in range(4):
            p = jnp.exp(parts[l] - lse)
            cut = slice(l * tok, (l + 1) * tok)
            dvt_ref[:, cut] += dot(grad_t, p.astype(BF16))
            probs.append(p)
            weighted.append(p * dot(grad, vt_ref[:, cut]))
        delta = jnp.sum(functools.reduce(jnp.add, weighted), axis=1, keepdims=True)
        dq = None
        for l in range(4):
            cut = slice(l * tok, (l + 1) * tok)
            ds = weighted[l] - probs[l] * delta
            at = tile_index(me, j, l)
            sums_ref[at] = sums_ref[at] + ds
            low = ds.astype(BF16)
            dkt_ref[:, cut] += dot(q_t, low)
            term = dot(low, proj_ref[1, 0, cut, :])
            dq = term if dq is None else dq + term
        dq = dq * 0.125
        dp_ref[rows, :width] = dq.astype(BF16)
        dpt_ref[j, :width, :] = dq.T.astype(BF16)
        return carry

    lax.fori_loop(0, 4, block, 0, unroll=4)
    dkt = dkt_ref[...]
    dvt = dvt_ref[...]
    dp_ref[:, width : 2 * width] = dkt.T.astype(BF16)
    dp_ref[:, 2 * width :] = dvt.T.astype(BF16)
    for j in range(4):
        cut = slice(j * tok, (j + 1) * tok)
        dpt_ref[j, width : 2 * width, :] = dkt[:, cut].astype(BF16)
        dpt_ref[j, 2 * width :, :] = dvt[:, cut].astype(BF16)

    strip = jnp.concatenate([sums_ref[1], sums_ref[2], sums_ref[3], jnp.zeros((tok, tok), F32)], axis=1)
    rows = tok
    while rows > 8:
        rows //= 2
        strip = strip[:rows] + pltpu.roll(strip[rows:], 4 * tok - rows, 1)
    diagonal = strip[0:1]
    for i in range(1, 8):
        diagonal = diagonal + pltpu.roll(strip[i : i + 1], 4 * tok - i, 1)
    col = lax.broadcasted_iota(jnp.int32, (1, 4 * tok), 1)
    bucket = bucket_of(col - tok - jnp.where(col >= 3 * tok, 4 * tok, 0))
    low_far = jnp.sum(jnp.sum(sums_ref[0], axis=0, keepdims=True), axis=1, keepdims=True)
    high_far = jnp.sum(jnp.sum(sums_ref[4], axis=0, keepdims=True), axis=1, keepdims=True)
    entry = lax.broadcasted_iota(jnp.int32, (BUCKETS, 1), 0)
    values = jnp.sum(jnp.where(bucket == entry, diagonal, 0.0), axis=1, keepdims=True)
    values = values + jnp.where(entry == 15, low_far, 0.0) + jnp.where(entry == 31, high_far, 0.0)
    lane = lax.broadcasted_iota(jnp.int32, (BUCKETS, D), 1) - me * (BUCKETS * heads)
    at = lax.broadcasted_iota(jnp.int32, (BUCKETS, D), 0) * heads + h
    table_row = jnp.sum(jnp.where(lane == at, values, 0.0), axis=0, keepdims=True)

    pieces = ((x0, 0, 0), (x1, 1, 0), (x2a, 2, 0), (x2b, 2, half), (x3a, 3, 0), (x3b, 3, half))
    total = None
    for ref, j, start in pieces:
        term = dot(dpt_ref[j, :, start : start + ref.shape[0]], ref[...])
        total = term if total is None else total + term
    payload_ref[...] = total.astype(BF16)
    gain_row = jnp.sum(total * w_ref[h].astype(F32), axis=0, keepdims=True) / gain_ref[...]
    row = lax.broadcasted_iota(jnp.int32, (8, D), 0)
    extra = jnp.where(row == 0, gain_row, jnp.where(row == 1, table_row, 0.0))
    extra_ref[...] = extra + extra_before[...] if h else extra
    if final:
        for j in range(4):
            cut = slice(j * tok, (j + 1) * tok)
            part = dot(dp_ref[cut, :], w_ref[h])
            for i, ref in enumerate((earlier, *dp_before)[: h]):
                part = part + dot(ref[cut, :], w_ref[i])
            if j % 2:
                normed_send_ref[j // 2] = part.astype(BF16)
            else:
                normed_near_ref[j // 2] = part
    else:
        dp_out[...] = dp_ref[...]


def hidden_units(rows_ref, grads_ref, w_in, w_out, active_ref, upward_ref):
    wide = 256
    count = rows_ref.shape[0] // 2
    c0, c1 = 0.7978845608028654, 0.044715
    for at in range(0, w_in.shape[1], wide):
        cut = slice(at, at + wide)
        for r in range(0, 2 * count, count):
            part = slice(r, r + count)
            v = dot(rows_ref[part, :], w_in[:, cut])
            square = v * v
            t = jnp.tanh(c0 * (v + c1 * (square * v)))
            half = 0.5 + 0.5 * t
            active_ref[part, cut] = (v * half).astype(BF16)
            slope = half + (0.5 * c0) * v * (1.0 - t * t) * (1.0 + (3.0 * c1) * square)
            grad = dot(grads_ref[part, :], w_out[cut, :], 1, 1)
            upward_ref[part, cut] = (grad * slope).astype(BF16)


def expert_own_kernel(
    near_ref, beside_ref, in_own, out_own, active_own, upward_own, rows_ref, grads_ref, sums_ref
):
    count = near_ref.shape[0]
    rows_ref[:count, :] = near_ref[:, :D]
    rows_ref[count:, :] = beside_ref[:, :D]
    grads_ref[:count, :] = near_ref[:, D:]
    grads_ref[count:, :] = beside_ref[:, D:]
    hidden_units(rows_ref, grads_ref, in_own, out_own, active_own, upward_own)
    wide = 256
    for at in range(0, D, wide):
        cut = slice(at, at + wide)
        into = slice(D + at, D + at + wide)
        for r in (0, count):
            part = slice(r, r + count)
            sums_ref[part, cut] = dot(active_own[part, :], out_own[:, cut])
            sums_ref[part, into] = dot(upward_own[part, :], in_own[cut, :], 1, 1)


def expert_far_kernel(
    far_a, far_b, far_c, out_a, out_b, rows_ref, grads_ref, sums_ref,
    in_grad_far, out_grad_far, mine_ref, theirs_ref, active_far, upward_far, in_far, out_far,
):
    count = mine_ref.shape[0]
    for whole, pieces in ((in_far, (far_a, far_b, far_c)), (out_far, (out_a, out_b))):
        at = 0
        for ref in pieces:
            whole[at : at + ref.shape[0], :] = ref[...]
            at += ref.shape[0]
    hidden_units(rows_ref, grads_ref, in_far, out_far, active_far, upward_far)
    wide = 256
    for at in range(0, D, wide):
        cut = slice(at, at + wide)
        into = slice(D + at, D + at + wide)
        for r in (count, 0):
            part = slice(r, r + count)
            produced = sums_ref[part, cut] + dot(active_far[part, :], out_far[:, cut])
            row_grad = sums_ref[part, into] + dot(upward_far[part, :], in_far[cut, :], 1, 1)
            if r:
                theirs_ref[:, cut] = produced.astype(BF16)
                theirs_ref[:, into] = row_grad.astype(BF16)
            else:
                mine_ref[:, cut] = produced
                mine_ref[:, into] = row_grad
        in_grad_far[:, cut] = dot(rows_ref[...], upward_far[:, cut], 0, 0).astype(BF16)
        out_grad_far[:, cut] = dot(active_far[...], grads_ref[:, cut], 0, 0).astype(BF16)


VMEM = pl.BlockSpec(memory_space=pltpu.VMEM)
SMEM = pl.BlockSpec(memory_space=pltpu.SMEM)
PARAMS = pltpu.CompilerParams(vmem_limit_bytes=24 * 1024 * 1024)


def halves(x, bit):
    n = x.shape[0] // 2
    upper = (lax.axis_index("expert") & bit) != 0
    keep = jnp.where(upper, x[n:], x[:n])
    send = jnp.where(upper, x[:n], x[n:])
    return keep, send


def add_low(a, b):
    return (a.astype(F32) + b.astype(F32)).astype(BF16)


def joined(x, other, bit):
    upper = (lax.axis_index("expert") & bit) != 0
    return jnp.concatenate([jnp.where(upper, other, x), jnp.where(upper, x, other)])


def shards(
    tokens,
    norm1_gain,
    qkv_weight,
    out_weight,
    bucket_position_bias,
    norm2_gain,
    router_weight,
    expert_in,
    expert_out,
    segment,
    route,
    slot,
    cotangent,
):
    highest_precision = lax.Precision.HIGHEST
    tok = tokens.shape[0]
    half = tok // 2
    seq = segment.shape[0]
    experts = router_weight.shape[1]
    capacity = (5 * tok + 4 * experts - 1) // (4 * experts)
    heads = bucket_position_bias.shape[1]
    width = out_weight.shape[0]
    me = lax.axis_index("shard").astype(jnp.int32).reshape(1)
    sources = lax.axis_size("expert")

    def over_x(v):
        return swap(v, "shard", 2)

    def over_core(v):
        return swap(v, "shard", 1)

    inputs = tokens.astype(F32)
    s1 = lax.rsqrt(jnp.mean(inputs * inputs, axis=-1, keepdims=True) + EPS)
    normed_low = (inputs * s1 * norm1_gain).astype(BF16)
    x2a = over_x(normed_low[:half])
    x2b = over_x(normed_low[half:])
    x1 = over_core(normed_low)
    x3a = over_core(x2a)
    x3b = over_core(x2b)
    pieces = (normed_low, x1, x2a, x2b, x3a, x3b)
    out_w1 = over_core(out_weight)
    out_w2 = over_x(out_weight)
    in_own, out_own = expert_in[0], expert_out[0]
    split = 13 * D // 24
    split_again = 3 * D // 4
    in_far = over_x(after(in_own[:split], x2b))
    qkv_t = jnp.transpose(qkv_weight.reshape(3, D, heads, HEAD_DIM), (2, 0, 3, 1))
    qkv_t = qkv_t.reshape(heads, 3 * HEAD_DIM, D)
    seg_rows = segment.reshape(4, 1, tok)
    seg_cols = segment.reshape(4, tok, 1)

    sds = jax.ShapeDtypeStruct
    proj, lse, *mixed = pl.pallas_call(
        forward_kernel,
        out_shape=[sds((3, heads, seq, HEAD_DIM), BF16), sds((heads, seq, 128), F32)]
        + [sds((tok, width), BF16)] * 4,
        in_specs=[SMEM, SMEM] + [VMEM] * 9,
        out_specs=[VMEM] * 6,
        scratch_shapes=[
            pltpu.VMEM((5, tok, tok), F32),
            pltpu.VMEM((heads, seq, HEAD_DIM), BF16),
            pltpu.VMEM((HEAD_DIM, seq), BF16),
        ],
        compiler_params=PARAMS,
        cost_estimate=pl.CostEstimate(flops=15 * 10**9, bytes_accessed=8 * 10**6, transcendentals=3 * 10**6),
        name="attention_forward",
    )(me, bucket_position_bias, seg_rows, seg_cols, *pieces, qkv_t.reshape(3 * width, D))

    *mixed, out_w2, in_far = lax.optimization_barrier((*mixed, out_w2, in_far))
    out_w3 = over_core(out_w2)
    out_w = jnp.concatenate([out_weight, out_w1, out_w2, out_w3])
    mixed_in = [swap(mixed[k], "shard", k) for k in (1, 2, 3)]
    in_rest = over_x(after(in_own[split:split_again], mixed_in[0]))
    in_last = over_x(after(in_own[split_again:], mixed_in[0]))
    split_out = 2 * D // 3
    out_far = over_x(after(out_own[:split_out], mixed_in[0]))
    mixed_own = jnp.concatenate([mixed[0]] + mixed_in, axis=1)
    attended = dot(mixed_own, out_w)
    hidden = inputs + attended
    s2 = lax.rsqrt(jnp.mean(hidden * hidden, axis=-1, keepdims=True) + EPS)
    routed_low = (hidden * s2 * norm2_gain).astype(BF16)
    routed_full = routed_low.astype(F32)
    chosen = (route[:, None] == jnp.arange(experts, dtype=jnp.int32)[None, :]).astype(F32)
    router_probs = jax.nn.softmax(jnp.dot(routed_full, router_weight, precision=highest_precision), axis=-1)
    gate = jnp.sum(router_probs * chosen, axis=-1, keepdims=True)
    upstream = cotangent.astype(F32)

    columns = jnp.arange(experts * capacity, dtype=jnp.int32)
    if sources == 8 == experts:
        order = jnp.repeat(jnp.asarray(ORDER, jnp.int32), capacity) ^ lax.axis_index("expert")
        columns = order * capacity + columns % capacity
    placed = ((route * capacity + slot)[:, None] == columns[None, :]) & (slot[:, None] >= 0)
    dispatch = placed.astype(BF16)
    both = jnp.concatenate([routed_low, (gate * upstream).astype(BF16)], axis=1)
    outgoing = dot(dispatch, both, 0, 0).astype(BF16)
    outgoing, in_rest = lax.optimization_barrier((outgoing, in_rest))
    arrived = exchange(outgoing)
    in_last, out_far, arrived = lax.optimization_barrier((in_last, out_far, arrived))
    out_last = over_x(after(out_own[split_out:], out_far))
    beside = over_core(arrived)
    count = experts * capacity

    active_own, upward_own, rows, grads, sums = pl.pallas_call(
        expert_own_kernel,
        out_shape=[sds((2 * count, D), BF16)] * 4 + [sds((2 * count, 2 * D), F32)],
        in_specs=[VMEM] * 4,
        out_specs=[VMEM] * 5,
        compiler_params=PARAMS,
        cost_estimate=pl.CostEstimate(flops=3 * 10**9, bytes_accessed=6 * 10**6, transcendentals=5 * 10**5),
        name="expert_own",
    )(arrived, beside, in_own, out_own)
    in_grad_far, out_grad_far, mine, theirs = pl.pallas_call(
        expert_far_kernel,
        out_shape=[sds((D, D), BF16)] * 2 + [sds((count, 2 * D), F32), sds((count, 2 * D), BF16)],
        in_specs=[VMEM] * 8,
        out_specs=[VMEM] * 4,
        scratch_shapes=[pltpu.VMEM((2 * count, D), BF16)] * 2 + [pltpu.VMEM((D, D), BF16)] * 2,
        compiler_params=PARAMS,
        cost_estimate=pl.CostEstimate(flops=5 * 10**9, bytes_accessed=6 * 10**6, transcendentals=5 * 10**5),
        name="expert_far",
    )(in_far, in_rest, in_last, out_far, out_last, rows, grads, sums)
    most = 5 * D // 6
    in_grad_rest = in_grad_far[most:]
    in_grad_far = over_x(in_grad_far[:most])
    returned = exchange(add_low(mine, over_core(theirs)))
    returned, in_grad_far = lax.optimization_barrier((returned, in_grad_far))
    back = dot(dispatch, returned)
    combined, expert_grad = back[:, :D], back[:, D:]
    output = (hidden + gate * combined).astype(BF16)
    gate_grad = jnp.sum(upstream * combined, axis=-1, keepdims=True)
    logit_grad = router_probs * (gate_grad * chosen - gate_grad * gate)
    router_grad = lax.dot_general(
        logit_grad, routed_full, (((0,), (0,)), ((), ())), precision=highest_precision
    )
    routed_grad = expert_grad + lax.dot_general(
        logit_grad, router_weight, (((1,), (1,)), ((), ())), precision=highest_precision
    )
    norm2_grad = jnp.sum(routed_grad * hidden * s2, axis=0, keepdims=True)
    scaled = routed_grad * norm2_gain
    hidden_grad = (
        upstream + s2 * scaled - hidden * s2**3 * jnp.mean(scaled * hidden, axis=-1, keepdims=True)
    )
    branch_low = hidden_grad.astype(BF16)
    mixed_grad = dot(branch_low, out_w, 1, 1).astype(BF16)
    mixed_grads = [mixed_grad[:, :width]] + [
        swap(mixed_grad[:, k * width : (k + 1) * width], "shard", k) for k in (1, 2, 3)
    ]
    branch1 = over_core(branch_low)
    branch2 = over_x(after(branch_low, mixed_grads[1]))
    in_grad_rest = over_x(after(in_grad_rest, mixed_grads[1]))
    def head_gradients(h, grads, earlier):
        final = h == heads - 1
        one = pl.BlockSpec((3, 1, seq, HEAD_DIM), lambda i: (0, h, 0, 0))
        log = pl.BlockSpec((1, seq, 128), lambda i: (h, 0, 0))
        return pl.pallas_call(
            functools.partial(backward_kernel, h, final),
            grid=(1,),
            out_shape=[sds((2, tok, D), F32), sds((2, tok, D), BF16)] * final
            + [sds((seq, 3 * HEAD_DIM), BF16)] * (not final)
            + [
                sds((3 * HEAD_DIM, D), BF16),
                sds((8, D), F32),
            ],
            in_specs=[SMEM, SMEM] + [VMEM] * 10 + [one, log] + [VMEM] * (4 + len(earlier)),
            out_specs=[VMEM] * (3 + final),
            scratch_shapes=[
                pltpu.VMEM((5, tok, tok), F32),
                pltpu.VMEM((5, tok, tok), F32),
                pltpu.VMEM((seq, HEAD_DIM), BF16),
                pltpu.VMEM((HEAD_DIM, seq), F32),
                pltpu.VMEM((HEAD_DIM, seq), F32),
                pltpu.VMEM((seq, 3 * HEAD_DIM), BF16),
                pltpu.VMEM((4, 3 * HEAD_DIM, tok), BF16),
                pltpu.VMEM((HEAD_DIM, seq), BF16),
                pltpu.VMEM((HEAD_DIM, seq), BF16),
            ],
            compiler_params=PARAMS,
            cost_estimate=pl.CostEstimate(flops=8 * 10**9, bytes_accessed=6 * 10**6, transcendentals=10**6),
            name="attention_backward_%d" % h,
        )(
            me, bucket_position_bias, seg_rows, seg_cols, *pieces, qkv_t, norm1_gain.reshape(1, D),
            proj, lse, *grads, *earlier,
        )

    in_step = sources == 8

    def scatter(part, bit):
        keep, send = halves(part, bit)
        return keep, swap(send, "expert", bit)

    dps, payloads, extra = [], [], None
    for h in range(heads):
        if h == heads - 1:
            mixed_grads[0], branch2, in_grad_rest = lax.optimization_barrier(
                (mixed_grads[0], branch2, in_grad_rest)
            )
            in_grad_far = jnp.concatenate([in_grad_far, in_grad_rest])
            early = 2 * D // 3
            out_grad_a = over_x(after(out_grad_far[:early], branch2))
            branch3 = over_core(branch2)
            branches = (branch_low, branch1, branch2, branch3)
            out_grad = sum(dot(mixed[k], b, 0, 0) for k, b in enumerate(branches))
            ahead = jnp.concatenate([payloads[0], out_grad.astype(BF16)])
            if in_step:
                keep, send = halves(ahead, 2)
                mixed_grads[0], keep, send = lax.optimization_barrier((mixed_grads[0], keep, send))
                other = swap(send, "expert", 2)
        earlier = []
        if h:
            earlier = [dps[0], extra]
        if h == heads - 1:
            earlier += dps[1:]
        *dp, payload, extra = head_gradients(h, mixed_grads, earlier)
        dps += dp
        payloads.append(payload)
    normed_near, normed_send = dps[-2:]
    small = jnp.concatenate([norm2_grad, router_grad])
    small = jnp.concatenate([small, extra[:2], jnp.zeros((-(experts + 3) % 16, D), F32)])
    count = small.shape[0]
    wide = jnp.concatenate(payloads[1:])
    normed_other = over_core(normed_send)

    def with_small(send, bit):
        got = swap(jnp.concatenate([send, small.astype(BF16)]), "expert", bit)
        return got[:-count], got[-count:].astype(F32)

    if in_step:
        ahead_keep, ahead_other = scatter(add_low(keep, other), 1)
        keep, send = halves(wide, 2)
        got, more = with_small(send, 2)
        got, more, ahead_other, normed_other, in_grad_far, out_grad_a = lax.optimization_barrier(
            (got, more, ahead_other, normed_other, in_grad_far, out_grad_a)
        )
        wide, small = add_low(keep, got), small + more
        ahead = add_low(ahead_keep, ahead_other)
    near = normed_near + normed_other.astype(F32)
    normed_other = over_x(near[1].astype(BF16))
    expert_in_grad = (dot(rows, upward_own, 0, 0) + in_grad_far.astype(F32))[None]
    if in_step:
        keep, send = halves(wide, 1)
        got, more = with_small(send, 1)
        ahead_other = swap(ahead, "expert", 4)
        got, more, ahead_other, normed_other, expert_in_grad = lax.optimization_barrier(
            (got, more, ahead_other, normed_other, expert_in_grad)
        )
        wide, small = add_low(keep, got), small + more
        ahead = add_low(ahead, ahead_other)
    normed_grad = near[0] + normed_other.astype(F32)
    scaled1 = normed_grad * norm1_gain
    input_grad = (
        hidden_grad
        + s1 * scaled1
        - inputs * s1**3 * jnp.mean(scaled1 * inputs, axis=-1, keepdims=True)
    )
    out_grad_b = over_x(after(out_grad_far[early:], normed_other))
    if in_step:
        got, more = with_small(wide, 4)
        ahead_other = swap(ahead, "expert", 1)
        got, more, ahead_other, input_grad, out_grad_b = lax.optimization_barrier(
            (got, more, ahead_other, input_grad, out_grad_b)
        )
        wide, small = add_low(wide, got), small + more
        ahead = joined(ahead, ahead_other, 1)
    else:
        wide, ahead, small = lax.psum((wide.astype(F32), ahead.astype(F32), small), "expert")
    small_other = over_x(small)
    out_grad_far = jnp.concatenate([out_grad_a, out_grad_b])
    expert_out_grad = (dot(active_own, grads, 0, 0) + out_grad_far.astype(F32))[None]
    if in_step:
        got, ahead_other = swap(wide, "expert", 1), swap(ahead, "expert", 2)
        got, ahead_other, small_other, expert_out_grad = lax.optimization_barrier(
            (got, ahead_other, small_other, expert_out_grad)
        )
        wide = joined(wide, got, 1)
        ahead = joined(ahead, ahead_other, 2)
    small = small + small_other
    small_other = over_core(small)
    if in_step:
        wide = joined(wide, swap(wide, "expert", 2), 2)
    small = small + small_other
    qkv_grad = jnp.concatenate([ahead[: 3 * HEAD_DIM], wide])
    qkv_grad = jnp.transpose(qkv_grad.reshape(heads, 3, HEAD_DIM, D), (1, 3, 0, 2))
    qkv_grad = qkv_grad.reshape(3, D, width).astype(F32)
    norm1_grad = small[experts + 1]
    table_size = BUCKETS * heads
    table_grad = lax.dynamic_slice_in_dim(small[experts + 2], me[0] * table_size, table_size)
    table_grad = table_grad.reshape(BUCKETS, heads)
    return (
        output,
        input_grad,
        norm1_grad,
        qkv_grad,
        ahead[3 * HEAD_DIM :].astype(F32),
        table_grad,
        small[0],
        jnp.transpose(small[1 : experts + 1]),
        expert_in_grad,
        expert_out_grad,
    )


def solution(mesh):
    placed = (
        P(("expert", "shard"), None),
        P(),
        P(None, None, "shard"),
        P("shard", None),
        P(None, "shard"),
        P(),
        P(),
        P("expert", None, "shard"),
        P("expert", "shard", None),
        P("expert"),
        P(("expert", "shard")),
        P(("expert", "shard")),
        P(("expert", "shard"), None),
    )
    return jax.shard_map(
        shards,
        mesh=mesh,
        in_specs=placed,
        out_specs=(
            P(("expert", "shard"), None),
            P(("expert", "shard"), None),
            P(),
            P(None, None, "shard"),
            P("shard", None),
            P(None, "shard"),
            P(),
            P(),
            P("expert", None, "shard"),
            P("expert", "shard", None),
        ),
        check_vma=False,
    )
```
